256 devices in a mesh: lat: 16 (over y_hi, z), lon: 16 (over x, y_lo, core).
Axes of the slice: x: 4, y: 4 (y_hi: 2, y_lo: 2; y = y_hi * 2 + y_lo), z: 8, core: 2. Of those that a mesh axis runs over, the one named last changes fastest.
Arguments:
- tokens: bfloat16 [192, 768, 4, 512], P('lat', 'lon'), may hold values from -100 to 240
- w_qkv: bfloat16 [2, 512, 1536], replicated, may hold values from -16 to 16
- w_out: bfloat16 [2, 512, 512], replicated, may hold values from -0.25 to 0.25
- modulation: float32 [2, 3, 512], replicated, may hold values from -2.5 to 2.5
- w_merge: bfloat16 [2048, 1024], replicated, may hold values from -0.125 to 0.125
Outputs:
- merged_tokens: bfloat16 [96, 384, 4, 1024], P('lat', 'lon')
The draws below stay inside these ranges and needn't reach their ends.
All inputs are finite; a program needn't handle non-finite values.
Results may differ from the reference program's by a relative error of at most 0.012.
Values may be sent and summed in bfloat16 or wider, within the bound.
No kernel may reach another device: no remote copies, remote signals or barrier semaphores. Data moves between devices by JAX's collectives and lax.ppermute only.
A program may use at most 128 MiB of HBM per device.

```python
import jax
import jax.numpy as jnp
from jax import lax

D = 512
HEADS = 16
WIN = 12
WLEV = 2
HALF = 6
LEV = 4
LAYERS = 2
NLAT = 192
NLON = 768


def draw_tokens(key, part):
    key = jax.random.fold_in(key, 11)
    shape = (NLAT, NLON, LEV, D)
    values = jax.random.truncated_normal(key, -6.0, 6.0, shape, jnp.float32)
    return values.astype(jnp.bfloat16)


def draw_w_qkv(key, part):
    key = jax.random.fold_in(key, 23)
    shape = (LAYERS, D, 3 * D)
    values = jax.random.truncated_normal(key, -6.0, 6.0, shape, jnp.float32) * D ** (-0.5)
    return values.astype(jnp.bfloat16)


def gaussian(key, extent, scale, reach, kind=jnp.bfloat16):
    return jnp.clip(scale * jax.random.normal(key, extent, jnp.float32), -reach, reach).astype(kind)


def setup_inputs(seed: int = 0) -> dict:
    key_of = jax.random.split(jax.random.key(seed), 6)
    return {
        "tokens": draw_tokens(jax.random.fold_in(key_of[5], 71), 0),
        "w_qkv": draw_w_qkv(jax.random.fold_in(key_of[5], 71), 0),
        "w_out": gaussian(key_of[2], (LAYERS, D, D), D ** -0.5, 0.25),
        "modulation": gaussian(key_of[3], (LAYERS, 3, D), 0.5, 2.5, jnp.float32),
        "w_merge": gaussian(key_of[4], (4 * D, 2 * D), (4 * D) ** -0.5, 0.125),
    }


def normalized(values, eps):
    centered = values - lax.optimization_barrier(jnp.mean(values, axis=-1, keepdims=True))
    return centered * lax.rsqrt(lax.optimization_barrier(jnp.mean(centered * centered, axis=-1, keepdims=True)) + eps)

def windowed(grid):
    rows, cols, depth, width = grid.shape
    parted = grid.reshape(rows // WIN, WIN, cols // WIN, WIN, depth // WLEV, WLEV, width)
    parted = parted.transpose(0, 2, 4, 1, 3, 5, 6)
    return parted.reshape(rows // WIN * (cols // WIN), depth // WLEV, WIN * WIN * WLEV, width)

def unwindowed(blocks, rows, cols, depth):
    width = blocks.shape[-1]
    parted = blocks.reshape(rows // WIN, cols // WIN, depth // WLEV, WIN, WIN, WLEV, width)
    return parted.transpose(0, 3, 1, 4, 2, 5, 6).reshape(rows, cols, depth, width)

def attend_block(hidden, residual, sides, wqkv, wout, gate):
    count, length, width = hidden.shape
    head_dim = width // HEADS
    packed = jnp.einsum('wtd,de->wte', hidden.astype(jnp.float32), wqkv.astype(jnp.float32)).astype(jnp.bfloat16)
    query = packed[..., :width].reshape(count, length, HEADS, head_dim)
    keys = packed[..., width:2 * width].reshape(count, length, HEADS, head_dim)
    values = packed[..., 2 * width:].reshape(count, length, HEADS, head_dim)
    scores = jnp.einsum('wqhd,wkhd->whqk', query.astype(jnp.float32), keys.astype(jnp.float32)) * head_dim ** (-0.5)
    allowed = (sides[:, :, None] == sides[:, None, :])[:, None]
    scores = jnp.where(allowed, scores, -1e+30)
    weights = jnp.exp(scores - lax.optimization_barrier(jnp.max(scores, axis=-1, keepdims=True)))
    weights = (weights / lax.optimization_barrier(jnp.sum(weights, axis=-1, keepdims=True))).astype(jnp.bfloat16)
    mixed = jnp.einsum('whqk,wkhd->wqhd', weights.astype(jnp.float32), values.astype(jnp.float32))
    mixed = mixed.astype(jnp.bfloat16).reshape(count, length, width)
    projected = jnp.einsum('wtd,de->wte', mixed.astype(jnp.float32), wout.astype(jnp.float32))
    return (residual.astype(jnp.float32) + (1.0 + gate) * projected).astype(jnp.bfloat16)

def window_layer(grid, side_grid, wqkv, wout, mod):
    rows, cols, depth, width = grid.shape
    hidden = (normalized(grid.astype(jnp.float32), 1e-06) * (1.0 + mod[0]) + mod[1]).astype(jnp.bfloat16)

    def one_block(items):
        return attend_block(items[0], items[1], items[2][..., 0], wqkv, wout, mod[2])
    blocks = lax.map(one_block, (windowed(hidden), windowed(grid), windowed(side_grid)))
    return unwindowed(blocks, rows, cols, depth)

def merged(grid, w_merge):
    rows, cols, depth, width = grid.shape
    joined = jnp.concatenate([grid[0::2, 0::2], grid[1::2, 0::2], grid[0::2, 1::2], grid[1::2, 1::2]], axis=-1)
    flat = normalized(joined.astype(jnp.float32).reshape(-1, 4 * width), 1e-05).astype(jnp.bfloat16)
    result = jnp.dot(flat, w_merge, preferred_element_type=jnp.float32).astype(jnp.bfloat16)
    return result.reshape(rows // 2, cols // 2, depth, 2 * width)

def reference(tokens, w_qkv, w_out, modulation, w_merge):
    rows = tokens.shape[0]
    plain = jnp.zeros(tokens.shape[:3] + (1,), jnp.int32)
    first = window_layer(tokens, plain, w_qkv[0], w_out[0], modulation[0])
    rolled = jnp.roll(first, (-HALF, -HALF), axis=(0, 1))
    anchor = (jnp.arange(rows, dtype=jnp.int32) + HALF) % rows
    sides = jnp.broadcast_to((anchor < HALF).astype(jnp.int32)[:, None, None, None], plain.shape)
    second = window_layer(rolled, sides, w_qkv[1], w_out[1], modulation[1])
    second = jnp.roll(second, (HALF, HALF), axis=(0, 1))
    return merged(second, w_merge)
```

```python
import functools
import math

import jax
import jax.numpy as jnp
from jax import lax
from jax.experimental import pallas as pl
from jax.experimental.pallas import tpu as pltpu
from jax.sharding import PartitionSpec as P

HEADS = 16
WIN = 12
HALF = 6
QUAD = 72
SPAN = 4 * QUAD
WIDTH = 512
HEAD = WIDTH // HEADS
GROUP = 8
MAIN = 256
REST = SPAN - MAIN
SUB = 18
FAR = -1e30
SCALE = math.log2(math.e) / math.sqrt(HEAD)
NT = (((1,), (1,)), ((), ()))


def dot(a, b):
    return jnp.dot(a, b, preferred_element_type=jnp.float32)


def dot_nt(a, b):
    return lax.dot_general(a, b, NT, preferred_element_type=jnp.float32)


def normalized(values, eps):
    centered = values - jnp.mean(values, axis=-1, keepdims=True)
    return centered * lax.rsqrt(jnp.mean(centered * centered, axis=-1, keepdims=True) + eps)


def softened(scores, apart, straddles):
    half = SPAN // 2
    top, bottom = scores[:half], scores[half:]
    if apart is None:
        most = jnp.maximum(jnp.max(top, axis=0, keepdims=True), jnp.max(bottom, axis=0, keepdims=True))
        return jnp.exp2(scores - most).astype(jnp.bfloat16)
    if straddles:
        lane = lax.broadcasted_iota(jnp.int32, (1, MAIN), 1)
        from_top = jnp.where(lane < half, 0.0, apart)
        from_bottom = jnp.where(lane < half, apart, 0.0)
    else:
        from_top = jnp.full((1, MAIN), apart, jnp.float32)
        from_bottom = jnp.zeros((1, MAIN), jnp.float32)
    most = jnp.maximum(
        jnp.max(top, axis=0, keepdims=True) + from_top, jnp.max(bottom, axis=0, keepdims=True) + from_bottom
    )
    return jnp.concatenate(
        [
            jnp.exp2(top - (most - from_top)).astype(jnp.bfloat16),
            jnp.exp2(bottom - (most - from_bottom)).astype(jnp.bfloat16),
        ],
        axis=0,
    )


def attend_window(grid, wqk_ref, wvt_ref, wout_ref, mod_ref, vt_ref, att_ref, apart):
    hidden = (normalized(grid, 1e-06) * (1.0 + mod_ref[0:1]) + mod_ref[1:2]).astype(jnp.bfloat16)
    query = (dot(hidden, wqk_ref[:, :WIDTH]) * SCALE).astype(jnp.bfloat16)
    keys = dot(hidden, wqk_ref[:, WIDTH:]).astype(jnp.bfloat16)
    vt_ref[...] = dot_nt(wvt_ref[...], hidden).astype(jnp.bfloat16)
    ones = jnp.ones((16, SPAN), jnp.bfloat16)
    wide = GROUP * HEAD
    lane_head = lax.broadcasted_iota(jnp.int32, (1, wide), 1) // HEAD
    same = (
        lax.broadcasted_iota(jnp.int32, (wide, wide), 0) // HEAD
        == lax.broadcasted_iota(jnp.int32, (wide, wide), 1) // HEAD
    )
    fold = (
        lax.broadcasted_iota(jnp.int32, (REST, wide), 0) == lax.broadcasted_iota(jnp.int32, (REST, wide), 1) % HEAD
    ).astype(jnp.bfloat16)
    eye = (
        lax.broadcasted_iota(jnp.int32, (MAIN, MAIN), 0) == lax.broadcasted_iota(jnp.int32, (MAIN, MAIN), 1)
    ).astype(jnp.bfloat16)
    rest = []
    for group in range(HEADS // GROUP):
        cols = slice(group * wide, (group + 1) * wide)
        qg, kg = query[:, cols], keys[:, cols]
        for item in range(GROUP):
            head = group * GROUP + item
            own = (lane_head == item).astype(jnp.bfloat16)
            weights = softened(dot_nt(kg, qg[:MAIN] * own), apart, True)
            mixed = dot(jnp.concatenate([vt_ref[head * HEAD : (head + 1) * HEAD], ones], axis=0), weights)
            att_ref[head * HEAD : (head + 1) * HEAD] = (mixed[:HEAD] * (1.0 / mixed[HEAD : HEAD + 1])).astype(
                jnp.bfloat16
            )
        spread = jnp.concatenate([qg[MAIN:]] * GROUP, axis=0) * same.astype(jnp.bfloat16)
        weights = softened(dot_nt(kg, spread), apart, False)
        mixed = dot(jnp.concatenate([vt_ref[cols], ones], axis=0), weights)
        mixed = jnp.where(same, mixed[:wide] * (1.0 / mixed[wide : wide + 1]), 0.0).astype(jnp.bfloat16)
        rest.append(dot_nt(fold, mixed).astype(jnp.bfloat16))
    main = dot_nt(eye, att_ref[...]).astype(jnp.bfloat16)
    attended = jnp.concatenate([main, jnp.concatenate(rest, axis=1)], axis=0)
    return grid + (1.0 + mod_ref[2:3]) * dot(attended, wout_ref[...])


def first_kernel(
    level, tokens_ref, wqk_ref, wvt_ref, wout_ref, mod_ref, up_ref, stay_top_ref, down_ref, stay_low_ref, west_ref,
    grid_ref, vt_ref, att_ref,
):
    window = pl.program_id(0)
    for quad in range(4):
        for sub in range(4):
            for place in range(9):
                i = quad // 2 * HALF + place // 3 * 2 + sub % 2
                j = quad % 2 * HALF + place % 3 * 2 + sub // 2
                row = quad * QUAD + sub * SUB + place * 2
                grid_ref[row : row + 2] = tokens_ref[i, j, level : level + 2].astype(jnp.float32)
    out = attend_window(grid_ref[...], wqk_ref, wvt_ref, wout_ref, mod_ref, vt_ref, att_ref, None)
    for side in range(2):
        block = 2 * window + side
        top = out[side * QUAD : (side + 1) * QUAD].astype(jnp.bfloat16)
        low = out[(2 + side) * QUAD : (3 + side) * QUAD].astype(jnp.bfloat16)
        stays = jnp.logical_and(block >= 1, block <= 4)

        @pl.when(stays)
        def _():
            stay_top_ref[block - 1] = top
            down_ref[block - 1] = low

        @pl.when(jnp.logical_not(stays))
        def _():
            up_ref[(block + 3) % 8] = top

        @pl.when(block >= 5)
        def _():
            stay_low_ref[block - 5] = low

        @pl.when(block == 0)
        def _():
            west_ref[0] = low


def second_kernel(
    apart_ref, stay_top_ref, above_ref, stay_low_ref, below_ref, east_low_ref, east_top_ref,
    wqk_ref, wvt_ref, wout_ref, mod_ref, merge_ref,
    back_up_ref, own_top_ref, own_low_ref, back_down_ref, back_east_ref,
    grid_ref, vt_ref, att_ref, joined_ref,
):
    window = pl.program_id(0)

    def put(quad, piece):
        grid_ref[quad * QUAD : (quad + 1) * QUAD] = piece.astype(jnp.float32)

    @pl.when(window < 2)
    def _():
        for side in range(2):
            put(side, above_ref[2 * window + side])
            put(2 + side, stay_top_ref[2 * window + side])

    @pl.when(window >= 2)
    def _():
        put(0, stay_low_ref[2 * window - 4])
        put(2, below_ref[2 * window - 4])

    @pl.when(window == 2)
    def _():
        put(1, stay_low_ref[1])
        put(3, below_ref[1])

    @pl.when(window == 3)
    def _():
        put(1, east_low_ref[0])
        put(3, east_top_ref[0])

    apart = jnp.where(window < 2, apart_ref[0], apart_ref[1])
    out = attend_window(grid_ref[...], wqk_ref, wvt_ref, wout_ref, mod_ref, vt_ref, att_ref, apart)
    grid_ref[...] = out.astype(jnp.bfloat16).astype(jnp.float32)
    for quad in range(4):
        for sub in range(4):
            start = quad * QUAD + sub * SUB
            joined_ref[window, quad * SUB : (quad + 1) * SUB, sub * WIDTH : (sub + 1) * WIDTH] = grid_ref[
                start : start + SUB
            ]

    @pl.when(window == 3)
    def _():
        flat = jnp.concatenate([normalized(joined_ref[w], 1e-05).astype(jnp.bfloat16) for w in range(4)], axis=0)
        merged = dot(flat, merge_ref[...])

        def piece(w, quad):
            return merged[w * QUAD + quad * SUB : w * QUAD + (quad + 1) * SUB].astype(jnp.bfloat16)

        for w in range(2):
            for side in range(2):
                back_up_ref[2 * w + side] = piece(w, side)
                own_top_ref[2 * w + side] = piece(w, 2 + side)
        own_low_ref[0], own_low_ref[1], own_low_ref[2] = piece(2, 0), piece(2, 1), piece(3, 0)
        back_down_ref[0], back_down_ref[1] = piece(2, 2), piece(2, 3)
        back_down_ref[2], back_down_ref[3] = piece(3, 2), piece(3, 3)
        back_east_ref[0] = piece(3, 1)


def last_kernel(*refs):
    out_ref = refs[-1]
    for pair in range(2):
        own_top, own_low, from_below, from_above, corner, from_west = refs[6 * pair : 6 * pair + 6]
        sources = {(0, 0): (corner, 0), (1, 0): (from_west, 0)}
        for c in range(4):
            sources[0, c + 1], sources[1, c + 1] = (own_top, c), (from_below, c)
        for c in range(3):
            sources[0, c + 5], sources[1, c + 5] = (from_above, c), (own_low, c)
        for (half, block), (ref, index) in sources.items():
            for place in range(9):
                i, j = half * 3 + place // 3, block * 3 + place % 3
                out_ref[i, j, 2 * pair : 2 * pair + 2] = ref[index, 2 * place : 2 * place + 2]


def whole(*shape):
    return pl.BlockSpec(shape, lambda w: (0,) * len(shape))


def struct(*shape):
    return jax.ShapeDtypeStruct(shape, jnp.bfloat16)


LIMIT = 48 * 1024 * 1024
LAYER_SCRATCH = [
    pltpu.VMEM((SPAN, WIDTH), jnp.float32),
    pltpu.VMEM((WIDTH, SPAN), jnp.bfloat16),
    pltpu.VMEM((WIDTH, MAIN), jnp.bfloat16),
]
LAYER_SPECS = [whole(WIDTH, 2 * WIDTH), whole(WIDTH, WIDTH), whole(WIDTH, WIDTH), whole(3, WIDTH)]
LAYER_FLOPS = 2 * 4 * SPAN * (4 * WIDTH * WIDTH + 2 * 8 * SPAN * WIDTH)


def first_layer(level, tokens, layer):
    counts = (4, 4, 4, 3, 1)
    return pl.pallas_call(
        functools.partial(first_kernel, level),
        grid=(4,),
        in_specs=[pl.BlockSpec((WIN, WIN, 4, WIDTH), lambda w: (0, w, 0, 0))] + LAYER_SPECS,
        out_specs=[whole(n, QUAD, WIDTH) for n in counts],
        out_shape=[struct(n, QUAD, WIDTH) for n in counts],
        scratch_shapes=LAYER_SCRATCH,
        compiler_params=pltpu.CompilerParams(vmem_limit_bytes=LIMIT),
        cost_estimate=pl.CostEstimate(flops=LAYER_FLOPS, bytes_accessed=5 << 20, transcendentals=16 * 4 * SPAN * SPAN),
        name=f"layer0_level{level}",
    )(tokens, *layer)


def second_layer(apart, pieces, layer, w_merge):
    outs = (4, 4, 3, 4, 1)
    return pl.pallas_call(
        second_kernel,
        grid=(4,),
        in_specs=[pl.BlockSpec(memory_space=pltpu.SMEM)]
        + [whole(p.shape[0], QUAD, WIDTH) for p in pieces]
        + LAYER_SPECS
        + [whole(4 * WIDTH, 2 * WIDTH)],
        out_specs=[whole(n, SUB, 2 * WIDTH) for n in outs],
        out_shape=[struct(n, SUB, 2 * WIDTH) for n in outs],
        scratch_shapes=LAYER_SCRATCH + [pltpu.VMEM((4, QUAD, 4 * WIDTH), jnp.float32)],
        compiler_params=pltpu.CompilerParams(vmem_limit_bytes=LIMIT),
        cost_estimate=pl.CostEstimate(
            flops=LAYER_FLOPS + 2 * SPAN * 8 * WIDTH * WIDTH, bytes_accessed=8 << 20, transcendentals=16 * 4 * SPAN * SPAN
        ),
        name="layer1_merge",
    )(apart, *pieces, *layer, w_merge)


def moved(value, axis, steps):
    count = lax.axis_size(axis)
    return lax.ppermute(value, axis, [(source, (source + steps) % count) for source in range(count)])


def body(tokens, w_qkv, w_out, modulation, w_merge):
    wqk = w_qkv[:, :, : 2 * WIDTH]
    wvt = jnp.swapaxes(w_qkv[:, :, 2 * WIDTH :], 1, 2)
    layers = [(wqk[i], wvt[i], w_out[i], modulation[i]) for i in range(2)]
    lat, last = lax.axis_index("lat"), lax.axis_size("lat") - 1
    apart = jnp.where(jnp.stack([lat == 0, lat == last]), FAR, 0.0).astype(jnp.float32)
    firsts = [first_layer(level, tokens, layers[0]) for level in (0, 2)]
    seconds = []
    for up, stay_top, down, stay_low, west in firsts:
        below = moved(up, "lat", -1)
        above = moved(down, "lat", 1)
        east_low = moved(west, "lon", -1)
        east_top = moved(below[3:], "lon", -1)
        pieces = (stay_top, above, stay_low, below, east_low, east_top)
        seconds.append(second_layer(apart, pieces, layers[1], w_merge))
    placed = []
    for back_up, own_top, own_low, back_down, back_east in seconds:
        from_below = moved(back_up, "lat", -1)
        from_above = moved(back_down, "lat", 1)
        from_west = moved(back_east, "lon", 1)
        corner = moved(from_above[3:], "lon", 1)
        placed += [own_top, own_low, from_below, from_above, corner, from_west]
    rows, cols = tokens.shape[0] // 2, tokens.shape[1] // 2
    return pl.pallas_call(
        last_kernel,
        out_shape=struct(rows, cols, 4, 2 * WIDTH),
        compiler_params=pltpu.CompilerParams(vmem_limit_bytes=LIMIT),
        name="placing",
    )(*placed)


def solution(mesh):
    in_specs = (P("lat", "lon", None, None), P(), P(), P(), P())
    out_specs = P("lat", "lon", None, None)
    return jax.shard_map(body, mesh=mesh, in_specs=in_specs, out_specs=out_specs, check_vma=False)
```

```python
import functools
import math

import jax
import jax.numpy as jnp
from jax import lax
from jax.experimental import pallas as pl
from jax.experimental.pallas import tpu as pltpu
from jax.sharding import PartitionSpec as P

HEADS = 16
WIN = 12
HALF = 6
QUAD = 72
SPAN = 4 * QUAD
WIDTH = 512
HEAD = WIDTH // HEADS
GROUP = 8
MAIN = 256
REST = SPAN - MAIN
SUB = 18
WINDOWS = 4
FAR = -1e30
SCALE = math.log2(math.e) / math.sqrt(HEAD)
NT = (((1,), (1,)), ((), ()))


def dot(a, b):
    return jnp.dot(a, b, preferred_element_type=jnp.float32)


def dot_nt(a, b):
    return lax.dot_general(a, b, NT, preferred_element_type=jnp.float32)


def normalized(values, eps):
    centered = values - jnp.mean(values, axis=-1, keepdims=True)
    return centered * lax.rsqrt(jnp.mean(centered * centered, axis=-1, keepdims=True) + eps)


def softened(scores, apart, straddles):
    half = SPAN // 2
    top, bottom = scores[:half], scores[half:]
    if apart is None:
        most = jnp.maximum(jnp.max(top, axis=0, keepdims=True), jnp.max(bottom, axis=0, keepdims=True))
        return jnp.exp2(scores - most).astype(jnp.bfloat16)
    if straddles:
        lane = lax.broadcasted_iota(jnp.int32, (1, MAIN), 1)
        from_top = jnp.where(lane < half, 0.0, apart)
        from_bottom = jnp.where(lane < half, apart, 0.0)
    else:
        from_top = jnp.full((1, MAIN), apart, jnp.float32)
        from_bottom = jnp.zeros((1, MAIN), jnp.float32)
    most = jnp.maximum(
        jnp.max(top, axis=0, keepdims=True) + from_top, jnp.max(bottom, axis=0, keepdims=True) + from_bottom
    )
    return jnp.concatenate(
        [
            jnp.exp2(top - (most - from_top)).astype(jnp.bfloat16),
            jnp.exp2(bottom - (most - from_bottom)).astype(jnp.bfloat16),
        ],
        axis=0,
    )


def attend_windows(grid_ref, wqkv_ref, wout_ref, mod_ref, scratch, aparts):
    hidden_ref, query_ref, keys_ref, vt_ref, scores_ref, rest_ref, att_ref = scratch
    wide = GROUP * HEAD
    lane_head = lax.broadcasted_iota(jnp.int32, (1, wide), 1) // HEAD
    same = (
        lax.broadcasted_iota(jnp.int32, (wide, wide), 0) // HEAD
        == lax.broadcasted_iota(jnp.int32, (wide, wide), 1) // HEAD
    )
    fold = (
        lax.broadcasted_iota(jnp.int32, (REST, wide), 0) == lax.broadcasted_iota(jnp.int32, (REST, wide), 1) % HEAD
    ).astype(jnp.bfloat16)
    ones = jnp.ones((16, SPAN), jnp.bfloat16)

    def main_rows(w):
        return pl.ds(pl.multiple_of(w * MAIN, MAIN), MAIN)

    def rest_rows(w):
        return pl.ds(pl.multiple_of(WINDOWS * MAIN + w * REST, REST), REST)

    @pl.loop(0, WINDOWS)
    def _(w):
        hidden = (normalized(grid_ref[w], 1e-06) * (1.0 + mod_ref[0:1]) + mod_ref[1:2]).astype(jnp.bfloat16)
        hidden_ref[main_rows(w)] = hidden[:MAIN]
        hidden_ref[rest_rows(w)] = hidden[MAIN:]

    query_ref[...] = (dot(hidden_ref[...], wqkv_ref[:, :WIDTH]) * SCALE).astype(jnp.bfloat16)
    keys_ref[...] = dot(hidden_ref[...], wqkv_ref[:, WIDTH : 2 * WIDTH]).astype(jnp.bfloat16)
    values = dot_nt(wqkv_ref[:, 2 * WIDTH :].T, hidden_ref[...]).astype(jnp.bfloat16)
    for w in range(WINDOWS):
        vt_ref[w, :, :MAIN] = values[:, w * MAIN : (w + 1) * MAIN]
        vt_ref[w, :, MAIN:] = values[:, WINDOWS * MAIN + w * REST : WINDOWS * MAIN + (w + 1) * REST]

    @pl.loop(0, WINDOWS)
    def _(w):
        apart = None if aparts is None else jnp.where(w < 2, aparts[0], aparts[1])
        for group in range(HEADS // GROUP):
            cols = slice(group * wide, (group + 1) * wide)
            kg = jnp.concatenate([keys_ref[main_rows(w), cols], keys_ref[rest_rows(w), cols]], axis=0)
            qm, qr = query_ref[main_rows(w), cols], query_ref[rest_rows(w), cols]
            for part in range(2):
                items = range(part * GROUP // 2, (part + 1) * GROUP // 2)
                masked = jnp.concatenate([kg * (lane_head == item).astype(jnp.bfloat16) for item in items], axis=0)
                scores_ref[2 * group + part] = dot_nt(masked, qm)
            rest_ref[group] = dot_nt(kg, jnp.concatenate([qr] * GROUP, axis=0) * same.astype(jnp.bfloat16))
        rest = []
        for group in range(HEADS // GROUP):
            cols = slice(group * wide, (group + 1) * wide)
            for item in range(GROUP):
                heads = slice((group * GROUP + item) * HEAD, (group * GROUP + item + 1) * HEAD)
                start = item % (GROUP // 2) * SPAN
                scores = scores_ref[2 * group + item // (GROUP // 2), start : start + SPAN]
                weights = softened(scores, apart, True)
                mixed = dot(jnp.concatenate([vt_ref[w, heads], ones], axis=0), weights)
                att_ref[heads] = mixed[:HEAD] * (1.0 / mixed[HEAD : HEAD + 1])
            weights = softened(rest_ref[group], apart, False)
            mixed = dot(jnp.concatenate([vt_ref[w, cols], ones], axis=0), weights)
            mixed = jnp.where(same, mixed[:wide] * (1.0 / mixed[wide : wide + 1]), 0.0).astype(jnp.bfloat16)
            rest.append(dot_nt(fold, mixed).astype(jnp.bfloat16))
        hidden_ref[main_rows(w)] = att_ref[...].T.astype(jnp.bfloat16)
        hidden_ref[rest_rows(w)] = jnp.concatenate(rest, axis=1)

    added = (1.0 + mod_ref[2:3]) * dot(hidden_ref[...], wout_ref[...])
    for w in range(WINDOWS):
        grid_ref[w, :MAIN] += added[w * MAIN : (w + 1) * MAIN]
        grid_ref[w, MAIN:] += added[WINDOWS * MAIN + w * REST : WINDOWS * MAIN + (w + 1) * REST]


def first_kernel(
    level, tokens_ref, wqkv_ref, wout_ref, mod_ref, up_ref, corner_ref, stay_top_ref, down_ref, stay_low_ref, west_ref,
    grid_ref, *scratch,
):
    @pl.loop(0, WINDOWS)
    def _(w):
        for quad in range(4):
            for sub in range(4):
                for place in range(9):
                    i = quad // 2 * HALF + place // 3 * 2 + sub % 2
                    j = quad % 2 * HALF + place % 3 * 2 + sub // 2
                    row = quad * QUAD + sub * SUB + place * 2
                    grid_ref[w, row : row + 2] = tokens_ref[i, w * WIN + j, level : level + 2].astype(jnp.float32)

    attend_windows(grid_ref, wqkv_ref.at[0], wout_ref.at[0], mod_ref.at[0], scratch, None)
    for block in range(8):
        w, side = divmod(block, 2)
        top = grid_ref[w, side * QUAD : (side + 1) * QUAD].astype(jnp.bfloat16)
        low = grid_ref[w, (2 + side) * QUAD : (3 + side) * QUAD].astype(jnp.bfloat16)
        if 1 <= block <= 4:
            stay_top_ref[block - 1] = top
            down_ref[block - 1] = low
        else:
            (up_ref if block else corner_ref)[max(block - 5, 0)] = top
            (stay_low_ref if block else west_ref)[max(block - 5, 0)] = low


def second_kernel(
    apart_ref, stay_top_ref, above_ref, stay_low_ref, below_ref, east_low_ref, east_top_ref,
    wqkv_ref, wout_ref, mod_ref, merge_ref,
    back_up_ref, own_top_ref, own_low_ref, back_down_ref, back_east_ref, back_corner_ref,
    grid_ref, *scratch,
):
    *scratch, joined_ref = scratch
    sources = [
        [(above_ref, 0), (above_ref, 1), (stay_top_ref, 0), (stay_top_ref, 1)],
        [(above_ref, 2), (above_ref, 3), (stay_top_ref, 2), (stay_top_ref, 3)],
        [(stay_low_ref, 0), (stay_low_ref, 1), (below_ref, 0), (below_ref, 1)],
        [(stay_low_ref, 2), (east_low_ref, 0), (below_ref, 2), (east_top_ref, 0)],
    ]
    for w in range(WINDOWS):
        for quad, (ref, index) in enumerate(sources[w]):
            grid_ref[w, quad * QUAD : (quad + 1) * QUAD] = ref[index].astype(jnp.float32)
    aparts = (apart_ref[0], apart_ref[1])
    attend_windows(grid_ref, wqkv_ref.at[1], wout_ref.at[1], mod_ref.at[1], scratch, aparts)

    @pl.loop(0, WINDOWS)
    def _(w):
        for quad in range(4):
            for sub in range(4):
                start = quad * QUAD + sub * SUB
                joined_ref[w, quad * SUB : (quad + 1) * SUB, sub * WIDTH : (sub + 1) * WIDTH] = (
                    grid_ref[w, start : start + SUB].astype(jnp.bfloat16).astype(jnp.float32)
                )

    flat = jnp.concatenate([normalized(joined_ref[w], 1e-05).astype(jnp.bfloat16) for w in range(WINDOWS)], axis=0)
    merged = dot(flat, merge_ref[...])

    def piece(w, quad):
        return merged[w * QUAD + quad * SUB : w * QUAD + (quad + 1) * SUB].astype(jnp.bfloat16)

    for w in range(2):
        for side in range(2):
            back_up_ref[2 * w + side] = piece(w, side)
            own_top_ref[2 * w + side] = piece(w, 2 + side)
    own_low_ref[0], own_low_ref[1], own_low_ref[2] = piece(2, 0), piece(2, 1), piece(3, 0)
    back_down_ref[0], back_down_ref[1], back_down_ref[2] = piece(2, 2), piece(2, 3), piece(3, 2)
    back_east_ref[0], back_corner_ref[0] = piece(3, 1), piece(3, 3)


def last_kernel(*refs):
    out_ref = refs[-1]
    for pair in range(2):
        own_top, own_low, from_below, from_above, corner, from_west = refs[6 * pair : 6 * pair + 6]
        sources = {(0, 0): (corner, 0), (1, 0): (from_west, 0)}
        for c in range(4):
            sources[0, c + 1], sources[1, c + 1] = (own_top, c), (from_below, c)
        for c in range(3):
            sources[0, c + 5], sources[1, c + 5] = (from_above, c), (own_low, c)
        for (half, block), (ref, index) in sources.items():
            for place in range(9):
                i, j = half * 3 + place // 3, block * 3 + place % 3
                out_ref[i, j, 2 * pair : 2 * pair + 2] = ref[index, 2 * place : 2 * place + 2]


def whole(*shape):
    return pl.BlockSpec(shape, lambda: (0,) * len(shape))


def struct(*shape):
    return jax.ShapeDtypeStruct(shape, jnp.bfloat16)


LIMIT = 28 * 1024 * 1024
LAYER_SCRATCH = [
    pltpu.VMEM((WINDOWS, SPAN, WIDTH), jnp.float32),
    pltpu.VMEM((WINDOWS * SPAN, WIDTH), jnp.bfloat16),
    pltpu.VMEM((WINDOWS * SPAN, WIDTH), jnp.bfloat16),
    pltpu.VMEM((WINDOWS * SPAN, WIDTH), jnp.bfloat16),
    pltpu.VMEM((WINDOWS, WIDTH, SPAN), jnp.bfloat16),
    pltpu.VMEM((4, HEADS // 4 * SPAN, MAIN), jnp.float32),
    pltpu.VMEM((HEADS // GROUP, SPAN, MAIN), jnp.float32),
    pltpu.VMEM((WIDTH, MAIN), jnp.float32),
]


LAYER_SPECS = [whole(2, WIDTH, 3 * WIDTH), whole(2, WIDTH, WIDTH), whole(2, 3, WIDTH)]
LAYER_FLOPS = 2 * 4 * SPAN * (4 * WIDTH * WIDTH + 2 * 8 * SPAN * WIDTH)


def first_layer(level, tokens, layers):
    counts = (3, 1, 4, 4, 3, 1)
    return pl.pallas_call(
        functools.partial(first_kernel, level),
        in_specs=[whole(*tokens.shape)] + LAYER_SPECS,
        out_specs=[whole(n, QUAD, WIDTH) for n in counts],
        out_shape=[struct(n, QUAD, WIDTH) for n in counts],
        scratch_shapes=LAYER_SCRATCH,
        compiler_params=pltpu.CompilerParams(vmem_limit_bytes=LIMIT),
        cost_estimate=pl.CostEstimate(flops=LAYER_FLOPS, bytes_accessed=5 << 20, transcendentals=16 * 4 * SPAN * SPAN),
        name=f"layer0_level{level}",
    )(tokens, *layers)


def second_layer(apart, pieces, layers, w_merge):
    outs = (4, 4, 3, 3, 1, 1)
    return pl.pallas_call(
        second_kernel,
        in_specs=[pl.BlockSpec(memory_space=pltpu.SMEM)]
        + [whole(p.shape[0], QUAD, WIDTH) for p in pieces]
        + LAYER_SPECS
        + [whole(4 * WIDTH, 2 * WIDTH)],
        out_specs=[whole(n, SUB, 2 * WIDTH) for n in outs],
        out_shape=[struct(n, SUB, 2 * WIDTH) for n in outs],
        scratch_shapes=LAYER_SCRATCH + [pltpu.VMEM((4, QUAD, 4 * WIDTH), jnp.float32)],
        compiler_params=pltpu.CompilerParams(vmem_limit_bytes=LIMIT),
        cost_estimate=pl.CostEstimate(
            flops=LAYER_FLOPS + 2 * SPAN * 8 * WIDTH * WIDTH, bytes_accessed=8 << 20, transcendentals=16 * 4 * SPAN * SPAN
        ),
        name="layer1_merge",
    )(apart, *pieces, *layers, w_merge)


def moved(value, down, east):
    lats, lons = lax.axis_size("lat"), lax.axis_size("lon")
    pairs = [
        (lat * lons + lon, (lat + down) % lats * lons + (lon + east) % lons) for lat in range(lats) for lon in range(lons)
    ]
    return lax.ppermute(value, ("lat", "lon"), pairs)


def body(tokens, w_qkv, w_out, modulation, w_merge):
    layers = (w_qkv, w_out, modulation)
    lat, last = lax.axis_index("lat"), lax.axis_size("lat") - 1
    apart = jnp.where(jnp.stack([lat == 0, lat == last]), FAR, 0.0).astype(jnp.float32)
    firsts = [first_layer(level, tokens, layers) for level in (0, 2)]
    seconds = []
    for up, corner, stay_top, down, stay_low, west in firsts:
        pieces = (stay_top, moved(down, 1, 0), stay_low, moved(up, -1, 0), moved(west, 0, -1), moved(corner, -1, -1))
        seconds.append(second_layer(apart, pieces, layers, w_merge))
    placed = []
    for back_up, own_top, own_low, back_down, back_east, back_corner in seconds:
        placed += [
            own_top, own_low, moved(back_up, -1, 0), moved(back_down, 1, 0), moved(back_corner, 1, 1), moved(back_east, 0, 1)
        ]
    rows, cols = tokens.shape[0] // 2, tokens.shape[1] // 2
    return pl.pallas_call(
        last_kernel,
        out_shape=struct(rows, cols, 4, 2 * WIDTH),
        compiler_params=pltpu.CompilerParams(vmem_limit_bytes=LIMIT),
        name="placing",
    )(*placed)


def solution(mesh):
    in_specs = (P("lat", "lon", None, None), P(), P(), P(), P())
    out_specs = P("lat", "lon", None, None)
    return jax.shard_map(body, mesh=mesh, in_specs=in_specs, out_specs=out_specs, check_vma=False)
```

```python
import functools
import math

import jax
import jax.numpy as jnp
from jax import lax
from jax.experimental import pallas as pl
from jax.experimental.pallas import tpu as pltpu
from jax.sharding import PartitionSpec as P

HEADS = 16
WIN = 12
HALF = 6
QUAD = 72
SPAN = 4 * QUAD
WIDTH = 512
HEAD = WIDTH // HEADS
GROUP = 8
MAIN = 256
REST = SPAN - MAIN
SUB = 18
WINDOWS = 4
FAR = -1e30
SCALE = math.log2(math.e) / math.sqrt(HEAD)
NT = (((1,), (1,)), ((), ()))


def dot(a, b):
    return jnp.dot(a, b, preferred_element_type=jnp.float32)


def dot_nt(a, b):
    return lax.dot_general(a, b, NT, preferred_element_type=jnp.float32)


def normalized(values, eps):
    centered = values - jnp.mean(values, axis=-1, keepdims=True)
    return centered * lax.rsqrt(jnp.mean(centered * centered, axis=-1, keepdims=True) + eps)


def softened(scores, apart, straddles):
    half = SPAN // 2
    top, bottom = scores[:half], scores[half:]
    if apart is None:
        most = jnp.maximum(jnp.max(top, axis=0, keepdims=True), jnp.max(bottom, axis=0, keepdims=True))
        return jnp.exp2(scores - most).astype(jnp.bfloat16)
    if straddles:
        lane = lax.broadcasted_iota(jnp.int32, (1, MAIN), 1)
        from_top = jnp.where(lane < half, 0.0, apart)
        from_bottom = jnp.where(lane < half, apart, 0.0)
    else:
        from_top = jnp.full((1, MAIN), apart, jnp.float32)
        from_bottom = jnp.zeros((1, MAIN), jnp.float32)
    most = jnp.maximum(
        jnp.max(top, axis=0, keepdims=True) + from_top, jnp.max(bottom, axis=0, keepdims=True) + from_bottom
    )
    return jnp.concatenate(
        [
            jnp.exp2(top - (most - from_top)).astype(jnp.bfloat16),
            jnp.exp2(bottom - (most - from_bottom)).astype(jnp.bfloat16),
        ],
        axis=0,
    )


def attend_windows(fill, grid_ref, wqkv_ref, wout_ref, mod_ref, scratch, copies, apart):
    hidden_ref, query_ref, keys_ref, vt_ref, scores_ref, rest_ref, att_ref = scratch
    copy_qkv, copy_out = copies
    wide = GROUP * HEAD
    lane_head = lax.broadcasted_iota(jnp.int32, (1, wide), 1) // HEAD
    same = (
        lax.broadcasted_iota(jnp.int32, (wide, wide), 0) // HEAD
        == lax.broadcasted_iota(jnp.int32, (wide, wide), 1) // HEAD
    )
    fold = (
        lax.broadcasted_iota(jnp.int32, (REST, wide), 0) == lax.broadcasted_iota(jnp.int32, (REST, wide), 1) % HEAD
    ).astype(jnp.bfloat16)
    ones = jnp.ones((16, SPAN), jnp.bfloat16)

    def main_rows(w):
        return pl.ds(pl.multiple_of(w * MAIN, MAIN), MAIN)

    def rest_rows(w):
        return pl.ds(pl.multiple_of(WINDOWS * MAIN + w * REST, REST), REST)

    @pl.loop(0, WINDOWS)
    def _(w):
        fill(w)
        hidden = (normalized(grid_ref[w], 1e-06) * (1.0 + mod_ref[0:1]) + mod_ref[1:2]).astype(jnp.bfloat16)
        hidden_ref[main_rows(w)] = hidden[:MAIN]
        hidden_ref[rest_rows(w)] = hidden[MAIN:]

    copy_qkv.wait()
    query_ref[...] = (dot(hidden_ref[...], wqkv_ref[:, :WIDTH]) * SCALE).astype(jnp.bfloat16)
    keys_ref[...] = dot(hidden_ref[...], wqkv_ref[:, WIDTH : 2 * WIDTH]).astype(jnp.bfloat16)
    values = dot_nt(wqkv_ref[:, 2 * WIDTH :].T, hidden_ref[...]).astype(jnp.bfloat16)
    for w in range(WINDOWS):
        vt_ref[w, :, :MAIN] = values[:, w * MAIN : (w + 1) * MAIN]
        vt_ref[w, :, MAIN:] = values[:, WINDOWS * MAIN + w * REST : WINDOWS * MAIN + (w + 1) * REST]

    @pl.loop(0, WINDOWS)
    def _(w):
        for group in range(HEADS // GROUP):
            cols = slice(group * wide, (group + 1) * wide)
            kg = jnp.concatenate([keys_ref[main_rows(w), cols], keys_ref[rest_rows(w), cols]], axis=0)
            qm, qr = query_ref[main_rows(w), cols], query_ref[rest_rows(w), cols]
            for part in range(2):
                items = range(part * GROUP // 2, (part + 1) * GROUP // 2)
                masked = jnp.concatenate([kg * (lane_head == item).astype(jnp.bfloat16) for item in items], axis=0)
                scores_ref[2 * group + part] = dot_nt(masked, qm)
            rest_ref[group] = dot_nt(kg, jnp.concatenate([qr] * GROUP, axis=0) * same.astype(jnp.bfloat16))
        rest = []
        for group in range(HEADS // GROUP):
            cols = slice(group * wide, (group + 1) * wide)
            for item in range(GROUP):
                heads = slice((group * GROUP + item) * HEAD, (group * GROUP + item + 1) * HEAD)
                start = item % (GROUP // 2) * SPAN
                scores = scores_ref[2 * group + item // (GROUP // 2), start : start + SPAN]
                weights = softened(scores, apart, True)
                mixed = dot(jnp.concatenate([vt_ref[w, heads], ones], axis=0), weights)
                att_ref[heads] = mixed[:HEAD] * (1.0 / mixed[HEAD : HEAD + 1])
            weights = softened(rest_ref[group], apart, False)
            mixed = dot(jnp.concatenate([vt_ref[w, cols], ones], axis=0), weights)
            mixed = jnp.where(same, mixed[:wide] * (1.0 / mixed[wide : wide + 1]), 0.0).astype(jnp.bfloat16)
            rest.append(dot_nt(fold, mixed).astype(jnp.bfloat16))
        hidden_ref[main_rows(w)] = att_ref[...].T.astype(jnp.bfloat16)
        hidden_ref[rest_rows(w)] = jnp.concatenate(rest, axis=1)

    copy_out.wait()
    added = (1.0 + mod_ref[2:3]) * dot(hidden_ref[...], wout_ref[...])
    for w in range(WINDOWS):
        grid_ref[w, :MAIN] += added[w * MAIN : (w + 1) * MAIN]
        grid_ref[w, MAIN:] += added[WINDOWS * MAIN + w * REST : WINDOWS * MAIN + (w + 1) * REST]


def staged(layer, wqkv_hbm, wout_hbm, wqkv_ref, wout_ref, sems):
    copies = (
        pltpu.make_async_copy(wqkv_hbm.at[layer], wqkv_ref, sems.at[0]),
        pltpu.make_async_copy(wout_hbm.at[layer], wout_ref, sems.at[1]),
    )
    for copy in copies:
        copy.start()
    return copies


def first_kernel(
    pair, tokens_hbm, wqkv_hbm, wout_hbm, mod_ref, moving_hbm, staying_hbm, west_hbm, corner_hbm,
    grid_ref, *scratch,
):
    *scratch, wqkv_ref, wout_ref, sems, tokens_ref, pieces_ref, token_sems, piece_sems = scratch

    def brought(w):
        columns = pl.ds(w * WIN, WIN)
        return pltpu.make_async_copy(tokens_hbm.at[:, columns], tokens_ref.at[w], token_sems.at[w])

    for w in range(WINDOWS):
        brought(w).start()
    copies = staged(0, wqkv_hbm, wout_hbm, wqkv_ref, wout_ref, sems)

    def fill(w):
        brought(w).wait()
        for quad in range(4):
            for sub in range(4):
                for place in range(9):
                    i = quad // 2 * HALF + place // 3 * 2 + sub % 2
                    j = quad % 2 * HALF + place % 3 * 2 + sub // 2
                    row = quad * QUAD + sub * SUB + place * 2
                    grid_ref[w, row : row + 2] = tokens_ref[w, i, j, 2 * pair : 2 * pair + 2].astype(jnp.float32)

    attend_windows(fill, grid_ref, wqkv_ref, wout_ref, mod_ref.at[0], scratch, copies, None)
    for block in range(8):
        w, side = divmod(block, 2)
        for half in range(2):
            quad = 2 * half + side
            pieces_ref[half, block] = grid_ref[w, quad * QUAD : (quad + 1) * QUAD].astype(jnp.bfloat16)
    out = pieces_ref.at[pair], pieces_ref.at[1 - pair]
    ends = [
        pltpu.make_async_copy(source, target, piece_sems.at[index])
        for index, (source, target) in enumerate(
            [
                (out[0].at[pl.ds(1, 7)], moving_hbm),
                (out[1].at[pl.ds(1, 7)], staying_hbm),
                (out[1].at[pl.ds(0, 1)], west_hbm),
                (out[0].at[pl.ds(0, 1)], corner_hbm),
            ]
        )
    ]
    for end in ends:
        end.start()
    for end in ends:
        end.wait()


def second_kernel(
    pair, apart_ref, staying_hbm, received_hbm, east_hbm, corner_hbm, wqkv_hbm, wout_hbm, mod_ref, merge_hbm,
    away_ref, own_ref, back_east_ref, back_corner_ref,
    grid_ref, *scratch,
):
    *scratch, wqkv_ref, wout_ref, sems, merge_ref, pieces_ref, joined_ref, merge_sem, piece_sems = scratch
    kept, got = pieces_ref.at[pair], pieces_ref.at[1 - pair]
    begins = [
        pltpu.make_async_copy(source, target, piece_sems.at[index])
        for index, (source, target) in enumerate(
            [
                (staying_hbm, kept.at[pl.ds(0, 7)]),
                (received_hbm, got.at[pl.ds(0, 7)]),
                (east_hbm, kept.at[pl.ds(7, 1)]),
                (corner_hbm, got.at[pl.ds(7, 1)]),
            ]
        )
    ]
    for begin in begins:
        begin.start()
    copies = staged(1, wqkv_hbm, wout_hbm, wqkv_ref, wout_ref, sems)
    copy_merge = pltpu.make_async_copy(merge_hbm, merge_ref, merge_sem)
    copy_merge.start()
    for begin in begins:
        begin.wait()

    def fill(w):
        for quad in range(4):
            grid_ref[w, quad * QUAD : (quad + 1) * QUAD] = pieces_ref[quad // 2, 2 * w + quad % 2].astype(jnp.float32)

    attend_windows(fill, grid_ref, wqkv_ref, wout_ref, mod_ref.at[1], scratch, copies, apart_ref[pair])

    @pl.loop(0, WINDOWS)
    def _(w):
        for quad in range(4):
            for sub in range(4):
                start = quad * QUAD + sub * SUB
                joined_ref[w, quad * SUB : (quad + 1) * SUB, sub * WIDTH : (sub + 1) * WIDTH] = (
                    grid_ref[w, start : start + SUB].astype(jnp.bfloat16).astype(jnp.float32)
                )

    flat = jnp.concatenate([normalized(joined_ref[w], 1e-05).astype(jnp.bfloat16) for w in range(WINDOWS)], axis=0)
    copy_merge.wait()
    merged = dot(flat, merge_ref[...])
    for block in range(8):
        w, side = divmod(block, 2)
        for half in range(2):
            start = w * QUAD + (2 * half + side) * SUB
            piece = merged[start : start + SUB].astype(jnp.bfloat16)
            if half == pair:
                target, last = own_ref, back_east_ref
            else:
                target, last = away_ref, back_corner_ref
            if block < 7:
                target[block] = piece
            else:
                last[0] = piece


def last_kernel(*refs):
    out_ref = refs[-1]
    for pair in range(2):
        own, back, from_west, corner = refs[4 * pair : 4 * pair + 4]
        for half in range(2):
            for block in range(8):
                if half != pair:
                    ref = own if block else from_west
                else:
                    ref = back if block else corner
                for place in range(9):
                    i, j = half * 3 + place // 3, block * 3 + place % 3
                    out_ref[i, j, 2 * pair : 2 * pair + 2] = ref[max(block - 1, 0), 2 * place : 2 * place + 2]


def whole(*shape):
    return pl.BlockSpec(shape, lambda: (0,) * len(shape))


def struct(*shape):
    return jax.ShapeDtypeStruct(shape, jnp.bfloat16)


LIMIT = 36 * 1024 * 1024
HBM = pl.BlockSpec(memory_space=pltpu.HBM)
LAYER_SCRATCH = [
    pltpu.VMEM((WINDOWS, SPAN, WIDTH), jnp.float32),
    pltpu.VMEM((WINDOWS * SPAN, WIDTH), jnp.bfloat16),
    pltpu.VMEM((WINDOWS * SPAN, WIDTH), jnp.bfloat16),
    pltpu.VMEM((WINDOWS * SPAN, WIDTH), jnp.bfloat16),
    pltpu.VMEM((WINDOWS, WIDTH, SPAN), jnp.bfloat16),
    pltpu.VMEM((4, HEADS // 4 * SPAN, MAIN), jnp.float32),
    pltpu.VMEM((HEADS // GROUP, SPAN, MAIN), jnp.float32),
    pltpu.VMEM((WIDTH, MAIN), jnp.float32),
    pltpu.VMEM((WIDTH, 3 * WIDTH), jnp.bfloat16),
    pltpu.VMEM((WIDTH, WIDTH), jnp.bfloat16),
    pltpu.SemaphoreType.DMA((2,)),
]
LAYER_SPECS = [HBM, HBM, whole(2, 3, WIDTH)]
LAYER_FLOPS = 2 * 4 * SPAN * (4 * WIDTH * WIDTH + 2 * 8 * SPAN * WIDTH)
COUNTS = (7, 7, 1, 1)


def first_layer(pair, tokens, layers):
    return pl.pallas_call(
        functools.partial(first_kernel, pair),
        in_specs=[HBM] + LAYER_SPECS,
        out_specs=[HBM] * 4,
        out_shape=[struct(n, QUAD, WIDTH) for n in COUNTS],
        scratch_shapes=LAYER_SCRATCH
        + [
            pltpu.VMEM((WINDOWS, WIN, WIN, 4, WIDTH), jnp.bfloat16),
            pltpu.VMEM((2, 8, QUAD, WIDTH), jnp.bfloat16),
            pltpu.SemaphoreType.DMA((WINDOWS,)),
            pltpu.SemaphoreType.DMA((4,)),
        ],
        compiler_params=pltpu.CompilerParams(vmem_limit_bytes=LIMIT),
        cost_estimate=pl.CostEstimate(flops=LAYER_FLOPS, bytes_accessed=5 << 20, transcendentals=16 * 4 * SPAN * SPAN),
        name=f"layer0_pair{pair}",
    )(tokens, *layers)


def second_layer(pair, apart, pieces, layers, w_merge):
    return pl.pallas_call(
        functools.partial(second_kernel, pair),
        in_specs=[pl.BlockSpec(memory_space=pltpu.SMEM)] + [HBM] * 4 + LAYER_SPECS + [HBM],
        out_specs=[whole(n, SUB, 2 * WIDTH) for n in COUNTS],
        out_shape=[struct(n, SUB, 2 * WIDTH) for n in COUNTS],
        scratch_shapes=LAYER_SCRATCH
        + [
            pltpu.VMEM((4 * WIDTH, 2 * WIDTH), jnp.bfloat16),
            pltpu.VMEM((2, 8, QUAD, WIDTH), jnp.bfloat16),
            pltpu.VMEM((4, QUAD, 4 * WIDTH), jnp.float32),
            pltpu.SemaphoreType.DMA(()),
            pltpu.SemaphoreType.DMA((4,)),
        ],
        compiler_params=pltpu.CompilerParams(vmem_limit_bytes=LIMIT),
        cost_estimate=pl.CostEstimate(
            flops=LAYER_FLOPS + 2 * SPAN * 8 * WIDTH * WIDTH, bytes_accessed=8 << 20, transcendentals=16 * 4 * SPAN * SPAN
        ),
        name=f"layer1_pair{pair}",
    )(apart, *pieces, *layers, w_merge)


def moved(value, down, east):
    lats, lons = lax.axis_size("lat"), lax.axis_size("lon")
    pairs = [
        (lat * lons + lon, (lat + down) % lats * lons + (lon + east) % lons) for lat in range(lats) for lon in range(lons)
    ]
    return lax.ppermute(value, ("lat", "lon"), pairs)


def body(tokens, w_qkv, w_out, modulation, w_merge):
    layers = (w_qkv, w_out, modulation)
    lat, last = lax.axis_index("lat"), lax.axis_size("lat") - 1
    apart = jnp.where(jnp.stack([lat == last, lat == 0]), FAR, 0.0).astype(jnp.float32)
    firsts = [first_layer(pair, tokens, layers) for pair in range(2)]
    seconds = []
    for pair, (moving, staying, west, corner) in enumerate(firsts):
        way = 2 * pair - 1
        pieces = (staying, moved(moving, way, 0), moved(west, 0, -1), moved(corner, way, -1))
        seconds.append(second_layer(pair, apart, pieces, layers, w_merge))
    placed = []
    for pair, (away, own, east, corner) in enumerate(seconds):
        way = 1 - 2 * pair
        placed += [own, moved(away, way, 0), moved(east, 0, 1), moved(corner, way, 1)]
    rows, cols = tokens.shape[0] // 2, tokens.shape[1] // 2
    return pl.pallas_call(
        last_kernel,
        out_shape=struct(rows, cols, 4, 2 * WIDTH),
        compiler_params=pltpu.CompilerParams(vmem_limit_bytes=LIMIT),
        name="placing",
    )(*placed)


def solution(mesh):
    in_specs = (P("lat", "lon", None, None), P(), P(), P(), P())
    out_specs = P("lat", "lon", None, None)
    return jax.shard_map(body, mesh=mesh, in_specs=in_specs, out_specs=out_specs, check_vma=False)
```

```python
import functools
import math

import jax
import jax.numpy as jnp
from jax import lax
from jax.experimental import pallas as pl
from jax.experimental.pallas import tpu as pltpu
from jax.sharding import PartitionSpec as P

HEADS = 16
WIN = 12
HALF = 6
QUAD = 72
SPAN = 4 * QUAD
WIDTH = 512
HEAD = WIDTH // HEADS
GROUP = 8
MAIN = 256
REST = SPAN - MAIN
SUB = 18
WINDOWS = 4
FAR = -1e30
SCALE = math.log2(math.e) / math.sqrt(HEAD)
NT = (((1,), (1,)), ((), ()))


def dot(a, b):
    return jnp.dot(a, b, preferred_element_type=jnp.float32)


def dot_nt(a, b):
    return lax.dot_general(a, b, NT, preferred_element_type=jnp.float32)


def normalized(values, eps):
    centered = values - jnp.mean(values, axis=-1, keepdims=True)
    return centered * lax.rsqrt(jnp.mean(centered * centered, axis=-1, keepdims=True) + eps)


def softened(scores, apart, straddles):
    half = SPAN // 2
    top, bottom = scores[:half], scores[half:]
    most_top, most_bottom = jnp.max(top, axis=0, keepdims=True), jnp.max(bottom, axis=0, keepdims=True)
    if apart is None:
        most_top = most_bottom = jnp.maximum(most_top, most_bottom)
    else:
        if straddles:
            lane = lax.broadcasted_iota(jnp.int32, (1, MAIN), 1)
            from_top = jnp.where(lane < half, 0.0, apart)
            from_bottom = jnp.where(lane < half, apart, 0.0)
        else:
            from_top = jnp.full((1, MAIN), apart, jnp.float32)
            from_bottom = jnp.zeros((1, MAIN), jnp.float32)
        most = jnp.maximum(most_top + from_top, most_bottom + from_bottom)
        most_top, most_bottom = most - from_top, most - from_bottom
    top, bottom = jnp.exp2(top - most_top), jnp.exp2(bottom - most_bottom)
    total = jnp.sum(top, axis=0, keepdims=True) + jnp.sum(bottom, axis=0, keepdims=True)
    return jnp.concatenate([top.astype(jnp.bfloat16), bottom.astype(jnp.bfloat16)], axis=0), 1.0 / total


def attend_windows(fill, finish, grid_ref, wqkv_ref, wout_ref, mod_ref, scratch, copies, apart):
    hidden_ref, query_ref, keys_ref, vt_ref, scores_ref, rest_ref, att_ref = scratch
    copy_qkv, copy_out = copies
    wide = GROUP * HEAD
    lane_head = lax.broadcasted_iota(jnp.int32, (1, wide), 1) // HEAD
    same = (
        lax.broadcasted_iota(jnp.int32, (wide, wide), 0) // HEAD
        == lax.broadcasted_iota(jnp.int32, (wide, wide), 1) // HEAD
    )

    def main_rows(w):
        return pl.ds(pl.multiple_of(w * MAIN, MAIN), MAIN)

    def rest_rows(w):
        return pl.ds(pl.multiple_of(WINDOWS * MAIN + w * REST, REST), REST)

    @pl.loop(0, WINDOWS)
    def _(w):
        fill(w)
        hidden = (normalized(grid_ref[w], 1e-06) * (1.0 + mod_ref[0]) + mod_ref[1]).astype(jnp.bfloat16)
        hidden_ref[main_rows(w)] = hidden[:MAIN]
        hidden_ref[rest_rows(w)] = hidden[MAIN:]

    copy_qkv.wait()
    query_ref[...] = (dot(hidden_ref[...], wqkv_ref[:, :WIDTH]) * SCALE).astype(jnp.bfloat16)
    keys_ref[...] = dot(hidden_ref[...], wqkv_ref[:, WIDTH : 2 * WIDTH]).astype(jnp.bfloat16)
    values = dot_nt(wqkv_ref[:, 2 * WIDTH :].T, hidden_ref[...]).astype(jnp.bfloat16)
    for w in range(WINDOWS):
        vt_ref[w, :, :MAIN] = values[:, w * MAIN : (w + 1) * MAIN]
        vt_ref[w, :, MAIN:] = values[:, WINDOWS * MAIN + w * REST : WINDOWS * MAIN + (w + 1) * REST]

    @pl.loop(0, WINDOWS)
    def _(w):
        for group in range(HEADS // GROUP):
            cols = slice(group * wide, (group + 1) * wide)
            kg = jnp.concatenate([keys_ref[main_rows(w), cols], keys_ref[rest_rows(w), cols]], axis=0)
            qm, qr = query_ref[main_rows(w), cols], query_ref[rest_rows(w), cols]
            for part in range(2):
                items = range(part * GROUP // 2, (part + 1) * GROUP // 2)
                masked = jnp.concatenate([kg * (lane_head == item).astype(jnp.bfloat16) for item in items], axis=0)
                scores_ref[2 * group + part] = dot_nt(masked, qm)
            rest_ref[group] = dot_nt(kg, jnp.concatenate([qr] * GROUP, axis=0) * same.astype(jnp.bfloat16))
        rest = []
        for group in range(HEADS // GROUP):
            cols = slice(group * wide, (group + 1) * wide)
            for item in range(GROUP):
                heads = slice((group * GROUP + item) * HEAD, (group * GROUP + item + 1) * HEAD)
                start = item % (GROUP // 2) * SPAN
                scores = scores_ref[2 * group + item // (GROUP // 2), start : start + SPAN]
                weights, share = softened(scores, apart, True)
                att_ref[heads] = dot(vt_ref[w, heads], weights) * share
            weights, share = softened(rest_ref[group], apart, False)
            mixed = dot(vt_ref[w, cols], weights) * share
            own = [slice(item * HEAD, (item + 1) * HEAD) for item in range(GROUP)]
            rest.append(jnp.concatenate([mixed[part, part] for part in own], axis=0).T.astype(jnp.bfloat16))
        hidden_ref[main_rows(w)] = att_ref[...].T.astype(jnp.bfloat16)
        hidden_ref[rest_rows(w)] = jnp.concatenate(rest, axis=1)

    copy_out.wait()
    added = (1.0 + mod_ref[2]) * dot(hidden_ref[...], wout_ref[...])
    for w in range(WINDOWS):
        grid_ref[w, :MAIN] += added[w * MAIN : (w + 1) * MAIN]
        grid_ref[w, MAIN:] += added[WINDOWS * MAIN + w * REST : WINDOWS * MAIN + (w + 1) * REST]
        finish(w)


def staged(layer, wqkv_hbm, wout_hbm, wqkv_ref, wout_ref, sems):
    copies = (
        pltpu.make_async_copy(wqkv_hbm.at[layer], wqkv_ref, sems.at[0]),
        pltpu.make_async_copy(wout_hbm.at[layer], wout_ref, sems.at[1]),
    )
    for copy in copies:
        copy.start()
    return copies


def first_kernel(
    pair, tokens_hbm, wqkv_hbm, wout_hbm, mod_ref, *refs,
):
    if pair:
        first_west_hbm, *refs = refs
    moving_hbm, staying_hbm, west_hbm, corner_hbm, grid_ref, *scratch = refs
    *scratch, wqkv_ref, wout_ref, sems, tokens_ref, pieces_ref, token_sems, piece_sems, pass_sem = scratch
    ends = []
    if pair:
        ends.append(pltpu.make_async_copy(first_west_hbm, west_hbm.at[pl.ds(0, 1)], pass_sem))
        ends[-1].start()

    def brought(w):
        columns = pl.ds(w * WIN, WIN)
        return pltpu.make_async_copy(tokens_hbm.at[:, columns], tokens_ref.at[w], token_sems.at[w])

    for w in range(WINDOWS):
        brought(w).start()
    copies = staged(0, wqkv_hbm, wout_hbm, wqkv_ref, wout_ref, sems)

    def fill(w):
        brought(w).wait()
        for quad in range(4):
            for sub in range(4):
                for place in range(9):
                    i = quad // 2 * HALF + place // 3 * 2 + sub % 2
                    j = quad % 2 * HALF + place % 3 * 2 + sub // 2
                    row = quad * QUAD + sub * SUB + place * 2
                    grid_ref[w, row : row + 2] = tokens_ref[w, i, j, 2 * pair : 2 * pair + 2].astype(jnp.float32)

    def finish(w):
        for quad in range(4):
            half, block = quad // 2, 2 * w + quad % 2
            piece = pieces_ref.at[half, pl.ds(block, 1)]
            piece[0] = grid_ref[w, quad * QUAD : (quad + 1) * QUAD].astype(jnp.bfloat16)
            if block:
                target = (moving_hbm if half == pair else staying_hbm).at[pl.ds(block - 1, 1)]
            else:
                target = corner_hbm if half == pair else west_hbm.at[pl.ds(pair, 1)]
            ends.append(pltpu.make_async_copy(piece, target, piece_sems.at[half, block]))
            ends[-1].start()

    attend_windows(fill, finish, grid_ref, wqkv_ref, wout_ref, mod_ref.at[:, pl.ds(0, 1)], scratch, copies, None)
    for end in ends:
        end.wait()


def second_kernel(
    pair, apart_ref, staying_hbm, received_hbm, east_hbm, corner_hbm, wqkv_hbm, wout_hbm, mod_ref, merge_hbm, *refs,
):
    if pair:
        first_east_ref, *refs = refs
    away_ref, own_ref, back_east_ref, corner_ref, grid_ref, *scratch = refs
    if pair:
        back_east_ref[0] = first_east_ref[0]
    *scratch, wqkv_ref, wout_ref, sems, merge_ref, pieces_ref, joined_ref, merge_sem, piece_sems = scratch
    kept, got = pieces_ref.at[pair], pieces_ref.at[1 - pair]
    begins = [
        pltpu.make_async_copy(source, target, piece_sems.at[index])
        for index, (source, target) in enumerate(
            [
                (staying_hbm, kept.at[pl.ds(0, 7)]),
                (received_hbm, got.at[pl.ds(0, 7)]),
                (east_hbm.at[pl.ds(pair, 1)], kept.at[pl.ds(7, 1)]),
                (corner_hbm, got.at[pl.ds(7, 1)]),
            ]
        )
    ]
    for begin in begins:
        begin.start()
    copies = staged(1, wqkv_hbm, wout_hbm, wqkv_ref, wout_ref, sems)
    copy_merge = pltpu.make_async_copy(merge_hbm, merge_ref, merge_sem)
    copy_merge.start()
    for begin in begins:
        begin.wait()

    def fill(w):
        for quad in range(4):
            grid_ref[w, quad * QUAD : (quad + 1) * QUAD] = pieces_ref[quad // 2, 2 * w + quad % 2].astype(jnp.float32)

    def finish(w):
        for quad in range(4):
            for sub in range(4):
                start = quad * QUAD + sub * SUB
                joined_ref[w, quad * SUB : (quad + 1) * SUB, sub * WIDTH : (sub + 1) * WIDTH] = (
                    grid_ref[w, start : start + SUB].astype(jnp.bfloat16).astype(jnp.float32)
                )

    attend_windows(
        fill, finish, grid_ref, wqkv_ref, wout_ref, mod_ref.at[:, pl.ds(1, 1)], scratch, copies, apart_ref[pair]
    )
    flat = jnp.concatenate([normalized(joined_ref[w], 1e-05).astype(jnp.bfloat16) for w in range(WINDOWS)], axis=0)
    copy_merge.wait()
    merged = dot(flat, merge_ref[...])
    for block in range(8):
        w, side = divmod(block, 2)
        for half in range(2):
            start = w * QUAD + (2 * half + side) * SUB
            piece = merged[start : start + SUB].astype(jnp.bfloat16)
            if half == pair:
                target, last = own_ref, back_east_ref
            else:
                target, last = away_ref, corner_ref
            if block < 7:
                target[block] = piece
            else:
                last[last.shape[0] - 1] = piece


def last_kernel(*refs):
    count = len(refs) // 2 - 2
    sources, out_hbm, held, (out_ref, sems, out_sems) = refs[:count], refs[count], refs[count + 1 : -3], refs[-3:]
    copies = [pltpu.make_async_copy(*pair, sems.at[index]) for index, pair in enumerate(zip(sources, held))]
    for copy in copies:
        copy.start()
    for copy in copies:
        copy.wait()
    ends = []
    for half in range(2):
        for pair in range(2):
            own, back, corner = held[3 * pair : 3 * pair + 3]
            for block in range(8):
                if half != pair:
                    ref, index = (own, block - 1) if block else (held[-1], pair)
                else:
                    ref, index = (back, block - 1) if block else (corner, 0)
                for place in range(9):
                    i, j = half * 3 + place // 3, block * 3 + place % 3
                    out_ref[i, j, 2 * pair : 2 * pair + 2] = ref[index, 2 * place : 2 * place + 2]
        rows = pl.ds(half * 3, 3)
        ends.append(pltpu.make_async_copy(out_ref.at[rows], out_hbm.at[rows], out_sems.at[half]))
        ends[-1].start()
    for end in ends:
        end.wait()


def whole(*shape):
    return pl.BlockSpec(shape, lambda: (0,) * len(shape))


def struct(*shape):
    return jax.ShapeDtypeStruct(shape, jnp.bfloat16)


LIMIT = 64 * 1024 * 1024 - 64 * 1024
HBM = pl.BlockSpec(memory_space=pltpu.HBM)
LAYER_SCRATCH = [
    pltpu.VMEM((WINDOWS, SPAN, WIDTH), jnp.float32),
    pltpu.VMEM((WINDOWS * SPAN, WIDTH), jnp.bfloat16),
    pltpu.VMEM((WINDOWS * SPAN, WIDTH), jnp.bfloat16),
    pltpu.VMEM((WINDOWS * SPAN, WIDTH), jnp.bfloat16),
    pltpu.VMEM((WINDOWS, WIDTH, SPAN), jnp.bfloat16),
    pltpu.VMEM((4, HEADS // 4 * SPAN, MAIN), jnp.float32),
    pltpu.VMEM((HEADS // GROUP, SPAN, MAIN), jnp.float32),
    pltpu.VMEM((WIDTH, MAIN), jnp.float32),
    pltpu.VMEM((WIDTH, 3 * WIDTH), jnp.bfloat16),
    pltpu.VMEM((WIDTH, WIDTH), jnp.bfloat16),
    pltpu.SemaphoreType.DMA((2,)),
]
LAYER_SPECS = [HBM, HBM, whole(3, 2, WIDTH)]
LAYER_FLOPS = 2 * 4 * SPAN * (6 * WIDTH * WIDTH + 5 * 8 * SPAN * WIDTH)


def first_layer(pair, tokens, layers, passed):
    counts = (7, 7, 1 + len(passed), 1)
    return pl.pallas_call(
        functools.partial(first_kernel, pair),
        in_specs=[HBM] + LAYER_SPECS + [HBM] * len(passed),
        out_specs=[HBM] * 4,
        out_shape=[struct(n, QUAD, WIDTH) for n in counts],
        scratch_shapes=LAYER_SCRATCH
        + [
            pltpu.VMEM((WINDOWS, WIN, WIN, 4, WIDTH), jnp.bfloat16),
            pltpu.VMEM((2, 8, QUAD, WIDTH), jnp.bfloat16),
            pltpu.SemaphoreType.DMA((WINDOWS,)),
            pltpu.SemaphoreType.DMA((2, 8)),
            pltpu.SemaphoreType.DMA(()),
        ],
        compiler_params=pltpu.CompilerParams(vmem_limit_bytes=LIMIT),
        cost_estimate=pl.CostEstimate(flops=LAYER_FLOPS, bytes_accessed=5 << 20, transcendentals=16 * 4 * SPAN * SPAN),
        name=f"layer0_pair{pair}",
    )(tokens, *layers, *passed)


def second_layer(pair, apart, pieces, layers, w_merge, passed):
    counts = (7, 7, 1 + len(passed), 1)
    return pl.pallas_call(
        functools.partial(second_kernel, pair),
        in_specs=[pl.BlockSpec(memory_space=pltpu.SMEM)] + [HBM] * 4 + LAYER_SPECS + [HBM] + [whole(*p.shape) for p in passed],
        out_specs=[whole(n, SUB, 2 * WIDTH) for n in counts],
        out_shape=[struct(n, SUB, 2 * WIDTH) for n in counts],
        scratch_shapes=LAYER_SCRATCH
        + [
            pltpu.VMEM((4 * WIDTH, 2 * WIDTH), jnp.bfloat16),
            pltpu.VMEM((2, 8, QUAD, WIDTH), jnp.bfloat16),
            pltpu.VMEM((4, QUAD, 4 * WIDTH), jnp.float32),
            pltpu.SemaphoreType.DMA(()),
            pltpu.SemaphoreType.DMA((4,)),
        ],
        compiler_params=pltpu.CompilerParams(vmem_limit_bytes=LIMIT),
        cost_estimate=pl.CostEstimate(
            flops=LAYER_FLOPS + 2 * SPAN * 8 * WIDTH * WIDTH, bytes_accessed=8 << 20, transcendentals=16 * 4 * SPAN * SPAN
        ),
        name=f"layer1_pair{pair}",
    )(apart, *pieces, *layers, w_merge, *passed)


def moved(value, down, east):
    lats, lons = lax.axis_size("lat"), lax.axis_size("lon")
    pairs = [
        (lat * lons + lon, (lat + down) % lats * lons + (lon + east) % lons) for lat in range(lats) for lon in range(lons)
    ]
    return lax.ppermute(value, ("lat", "lon"), pairs)


def body(tokens, w_qkv, w_out, modulation, w_merge):
    layers = (w_qkv, w_out, jnp.swapaxes(modulation, 0, 1))
    lat, last = lax.axis_index("lat"), lax.axis_size("lat") - 1
    apart = jnp.where(jnp.stack([lat == last, lat == 0]), FAR, 0.0).astype(jnp.float32)
    firsts, passed = [], []
    for pair in range(2):
        firsts.append(first_layer(pair, tokens, layers, passed))
        passed = firsts[-1][2:3]
    beside = moved(passed[0], 0, -1)
    placed, passed = [], []
    for pair, (moving, staying, _, corner) in enumerate(firsts):
        way = 2 * pair - 1
        pieces = (staying, moved(moving, way, 0), beside, moved(corner, way, -1))
        away, own, east, corner = second_layer(pair, apart, pieces, layers, w_merge, passed)
        placed += [own, moved(away, -way, 0), moved(corner, -way, 1)]
        passed = [east]
    placed.append(moved(east, 0, 1))
    rows, cols = tokens.shape[0] // 2, tokens.shape[1] // 2
    return pl.pallas_call(
        last_kernel,
        in_specs=[HBM] * len(placed),
        out_specs=HBM,
        out_shape=struct(rows, cols, 4, 2 * WIDTH),
        scratch_shapes=[pltpu.VMEM(p.shape, p.dtype) for p in placed]
        + [
            pltpu.VMEM((rows, cols, 4, 2 * WIDTH), jnp.bfloat16),
            pltpu.SemaphoreType.DMA((len(placed),)),
            pltpu.SemaphoreType.DMA((2,)),
        ],
        compiler_params=pltpu.CompilerParams(vmem_limit_bytes=LIMIT),
        name="placing",
    )(*placed)


def solution(mesh):
    in_specs = (P("lat", "lon", None, None), P(), P(), P(), P())
    out_specs = P("lat", "lon", None, None)
    return jax.shard_map(body, mesh=mesh, in_specs=in_specs, out_specs=out_specs, check_vma=False)
```

```python
import functools
import math

import jax
import jax.numpy as jnp
from jax import lax
from jax.experimental import pallas as pl
from jax.experimental.pallas import tpu as pltpu
from jax.sharding import PartitionSpec as P

HEADS = 16
WIN = 12
HALF = 6
QUAD = 72
SPAN = 4 * QUAD
WIDTH = 512
HEAD = WIDTH // HEADS
GROUP = 8
MAIN = 256
REST = SPAN - MAIN
SUB = 18
WINDOWS = 4
BACK = 128
FAR = -1e30
SCALE = math.log2(math.e) / math.sqrt(HEAD)
NT = (((1,), (1,)), ((), ()))


def dot(a, b):
    return jnp.dot(a, b, preferred_element_type=jnp.float32)


def dot_nt(a, b):
    return lax.dot_general(a, b, NT, preferred_element_type=jnp.float32)


def normalized(values, eps):
    centered = values - jnp.mean(values, axis=-1, keepdims=True)
    return centered * lax.rsqrt(jnp.mean(centered * centered, axis=-1, keepdims=True) + eps)


def softened(scores, apart, straddles):
    half = SPAN // 2
    top, bottom = scores[:half], scores[half:]
    most_top, most_bottom = jnp.max(top, axis=0, keepdims=True), jnp.max(bottom, axis=0, keepdims=True)
    if apart is None:
        most_top = most_bottom = jnp.maximum(most_top, most_bottom)
    else:
        if straddles:
            lane = lax.broadcasted_iota(jnp.int32, (1, MAIN), 1)
            from_top = jnp.where(lane < half, 0.0, apart)
            from_bottom = jnp.where(lane < half, apart, 0.0)
        else:
            from_top = jnp.full((1, MAIN), apart, jnp.float32)
            from_bottom = jnp.zeros((1, MAIN), jnp.float32)
        most = jnp.maximum(most_top + from_top, most_bottom + from_bottom)
        most_top, most_bottom = most - from_top, most - from_bottom
    top, bottom = jnp.exp2(top - most_top), jnp.exp2(bottom - most_bottom)
    total = jnp.sum(top, axis=0, keepdims=True) + jnp.sum(bottom, axis=0, keepdims=True)
    return jnp.concatenate([top.astype(jnp.bfloat16), bottom.astype(jnp.bfloat16)], axis=0), 1.0 / total


def attend_windows(fill, finish, grid_ref, wqkv_ref, wout_ref, mod_ref, scratch, copies, apart):
    hidden_ref, query_ref, keys_ref, vt_ref, scores_ref, rest_ref, att_ref = scratch
    copy_qkv, copy_out = copies
    wide = GROUP * HEAD
    lane_head = lax.broadcasted_iota(jnp.int32, (1, wide), 1) // HEAD
    same = (
        lax.broadcasted_iota(jnp.int32, (wide, wide), 0) // HEAD
        == lax.broadcasted_iota(jnp.int32, (wide, wide), 1) // HEAD
    )

    def main_rows(w):
        return pl.ds(pl.multiple_of(w * MAIN, MAIN), MAIN)

    def rest_rows(w):
        return pl.ds(pl.multiple_of(WINDOWS * MAIN + w * REST, REST), REST)

    for w in range(WINDOWS):
        fill(w)
        hidden = (normalized(grid_ref[w], 1e-06) * (1.0 + mod_ref[0]) + mod_ref[1]).astype(jnp.bfloat16)
        hidden_ref[main_rows(w)] = hidden[:MAIN]
        hidden_ref[rest_rows(w)] = hidden[MAIN:]

    copy_qkv.wait()
    query_ref[...] = (dot(hidden_ref[...], wqkv_ref[:, :WIDTH]) * SCALE).astype(jnp.bfloat16)
    keys_ref[...] = dot(hidden_ref[...], wqkv_ref[:, WIDTH : 2 * WIDTH]).astype(jnp.bfloat16)
    values = dot_nt(wqkv_ref[:, 2 * WIDTH :].T, hidden_ref[...]).astype(jnp.bfloat16)
    for w in range(WINDOWS):
        vt_ref[w, :, :MAIN] = values[:, w * MAIN : (w + 1) * MAIN]
        vt_ref[w, :, MAIN:] = values[:, WINDOWS * MAIN + w * REST : WINDOWS * MAIN + (w + 1) * REST]

    def attend(w, scores_ref, rest_ref, att_ref):
        for group in range(HEADS // GROUP):
            cols = slice(group * wide, (group + 1) * wide)
            kg = jnp.concatenate([keys_ref[main_rows(w), cols], keys_ref[rest_rows(w), cols]], axis=0)
            qm, qr = query_ref[main_rows(w), cols], query_ref[rest_rows(w), cols]
            for part in range(2):
                items = range(part * GROUP // 2, (part + 1) * GROUP // 2)
                masked = jnp.concatenate([kg * (lane_head == item).astype(jnp.bfloat16) for item in items], axis=0)
                scores_ref[2 * group + part] = dot_nt(masked, qm)
            rest_ref[group] = dot_nt(kg, jnp.concatenate([qr] * GROUP, axis=0) * same.astype(jnp.bfloat16))
        rest = []
        for group in range(HEADS // GROUP):
            cols = slice(group * wide, (group + 1) * wide)
            for item in range(GROUP):
                heads = slice((group * GROUP + item) * HEAD, (group * GROUP + item + 1) * HEAD)
                start = item % (GROUP // 2) * SPAN
                scores = scores_ref[2 * group + item // (GROUP // 2), start : start + SPAN]
                weights, share = softened(scores, apart, True)
                att_ref[heads] = dot(vt_ref[w, heads], weights) * share
            weights, share = softened(rest_ref[group], apart, False)
            mixed = dot(vt_ref[w, cols], weights) * share
            own = [slice(item * HEAD, (item + 1) * HEAD) for item in range(GROUP)]
            rest.append(jnp.concatenate([mixed[part, part] for part in own], axis=0).T.astype(jnp.bfloat16))
        hidden_ref[main_rows(w)] = att_ref[...].T.astype(jnp.bfloat16)
        hidden_ref[rest_rows(w)] = jnp.concatenate(rest, axis=1)

    for w in range(WINDOWS):
        attend(w, scores_ref.at[w % 2], rest_ref.at[w % 2], att_ref.at[w % 2])

    copy_out.wait()
    added = (1.0 + mod_ref[2]) * dot(hidden_ref[...], wout_ref[...])
    for w in range(WINDOWS):
        grid_ref[w, :MAIN] += added[w * MAIN : (w + 1) * MAIN]
        grid_ref[w, MAIN:] += added[WINDOWS * MAIN + w * REST : WINDOWS * MAIN + (w + 1) * REST]
        finish(w)


def staged(layer, wqkv_hbm, wout_hbm, wqkv_ref, wout_ref, sems):
    copies = (
        pltpu.make_async_copy(wqkv_hbm.at[layer], wqkv_ref, sems.at[0]),
        pltpu.make_async_copy(wout_hbm.at[layer], wout_ref, sems.at[1]),
    )
    for copy in copies:
        copy.start()
    return copies


def first_kernel(
    pair, tokens_hbm, wqkv_hbm, wout_hbm, mod_ref, *refs,
):
    if pair:
        first_west_hbm, *refs = refs
    moving_hbm, staying_hbm, west_hbm, corner_hbm, grid_ref, *scratch = refs
    *scratch, wqkv_ref, wout_ref, sems, tokens_ref, pieces_ref, token_sems, piece_sems, pass_sem = scratch
    ends = []
    if pair:
        ends.append(pltpu.make_async_copy(first_west_hbm, west_hbm.at[pl.ds(0, 1)], pass_sem))
        ends[-1].start()

    def brought(w):
        columns = pl.ds(w * WIN, WIN)
        return pltpu.make_async_copy(tokens_hbm.at[:, columns], tokens_ref.at[w], token_sems.at[w])

    for w in range(WINDOWS):
        brought(w).start()
    copies = staged(0, wqkv_hbm, wout_hbm, wqkv_ref, wout_ref, sems)

    def fill(w):
        brought(w).wait()
        for quad in range(4):
            for sub in range(4):
                for place in range(9):
                    i = quad // 2 * HALF + place // 3 * 2 + sub % 2
                    j = quad % 2 * HALF + place % 3 * 2 + sub // 2
                    row = quad * QUAD + sub * SUB + place * 2
                    grid_ref[w, row : row + 2] = tokens_ref[w, i, j, 2 * pair : 2 * pair + 2].astype(jnp.float32)

    def finish(w):
        for quad in range(4):
            half, block = quad // 2, 2 * w + quad % 2
            piece = pieces_ref.at[half, pl.ds(block, 1)]
            piece[0] = grid_ref[w, quad * QUAD : (quad + 1) * QUAD].astype(jnp.bfloat16)
            if block:
                target = (moving_hbm if half == pair else staying_hbm).at[pl.ds(block - 1, 1)]
            else:
                target = corner_hbm if half == pair else west_hbm.at[pl.ds(pair, 1)]
            ends.append(pltpu.make_async_copy(piece, target, piece_sems.at[half, block]))
            ends[-1].start()

    attend_windows(fill, finish, grid_ref, wqkv_ref, wout_ref, mod_ref.at[:, pl.ds(0, 1)], scratch, copies, None)
    for end in ends:
        end.wait()


def second_kernel(
    pair, staying_hbm, received_hbm, east_hbm, corner_hbm, wqkv_hbm, wout_hbm, mod_ref, merge_hbm, *refs,
):
    if pair:
        first_east_ref, *refs = refs
    away_ref, own_ref, back_east_ref, corner_ref, grid_ref, *scratch = refs
    if pair:
        back_east_ref[0] = first_east_ref[0]
    *scratch, wqkv_ref, wout_ref, sems, merge_ref, pieces_ref, joined_ref, merge_sem, piece_sems = scratch
    kept, got = pieces_ref.at[pair], pieces_ref.at[1 - pair]
    begins = [
        pltpu.make_async_copy(source, target, piece_sems.at[index])
        for index, (source, target) in enumerate(
            [
                (staying_hbm, kept.at[pl.ds(0, 7)]),
                (received_hbm, got.at[pl.ds(0, 7)]),
                (east_hbm.at[pl.ds(pair, 1)], kept.at[pl.ds(7, 1)]),
                (corner_hbm, got.at[pl.ds(7, 1)]),
            ]
        )
    ]
    for begin in begins:
        begin.start()
    copies = staged(1, wqkv_hbm, wout_hbm, wqkv_ref, wout_ref, sems)
    copy_merge = pltpu.make_async_copy(merge_hbm, merge_ref, merge_sem)
    copy_merge.start()
    for begin in begins:
        begin.wait()

    def fill(w):
        for quad in range(4):
            grid_ref[w, quad * QUAD : (quad + 1) * QUAD] = pieces_ref[quad // 2, 2 * w + quad % 2].astype(jnp.float32)

    def finish(w):
        for quad in range(4):
            for sub in range(4):
                start = quad * QUAD + sub * SUB
                joined_ref[w, quad * SUB : (quad + 1) * SUB, sub * WIDTH : (sub + 1) * WIDTH] = (
                    grid_ref[w, start : start + SUB].astype(jnp.bfloat16).astype(jnp.float32)
                )

    border = 0 if pair else lax.axis_size("lat") - 1
    apart = jnp.where(lax.axis_index("lat") == border, FAR, 0.0)
    attend_windows(fill, finish, grid_ref, wqkv_ref, wout_ref, mod_ref.at[:, pl.ds(1, 1)], scratch, copies, apart)
    flat = jnp.concatenate([normalized(joined_ref[w], 1e-05).astype(jnp.bfloat16) for w in range(WINDOWS)], axis=0)
    copy_merge.wait()
    merged = dot(flat, merge_ref[...])
    for half in range(2):
        target, last = (own_ref, back_east_ref) if half == pair else (away_ref, corner_ref)
        rows = [merged[w * QUAD + 2 * half * SUB : w * QUAD + 2 * (half + 1) * SUB] for w in range(WINDOWS)]
        rows = jnp.concatenate(rows, axis=0)
        target[...] = rows[:BACK].astype(jnp.bfloat16)
        last[last.shape[0] - 1] = rows[7 * SUB :].astype(jnp.bfloat16)


def last_kernel(*refs):
    count = len(refs) // 2 - 2
    sources, out_hbm, held, (out_ref, sems, out_sems) = refs[:count], refs[count], refs[count + 1 : -3], refs[-3:]
    copies = [pltpu.make_async_copy(*pair, sems.at[index]) for index, pair in enumerate(zip(sources, held))]
    for copy in copies:
        copy.start()
    for copy in copies:
        copy.wait()
    ends = []
    for half in range(2):
        for pair in range(2):
            own, back, corner = held[3 * pair : 3 * pair + 3]
            for block in range(8):
                if half != pair:
                    ref = own if block else held[-1].at[pair]
                else:
                    ref = back if block else corner.at[0]
                for place in range(9):
                    i, j = half * 3 + place // 3, block * 3 + place % 3
                    row = max(block - 1, 0) * SUB + 2 * place
                    out_ref[i, j, 2 * pair : 2 * pair + 2] = ref[row : row + 2]
        rows = pl.ds(half * 3, 3)
        ends.append(pltpu.make_async_copy(out_ref.at[rows], out_hbm.at[rows], out_sems.at[half]))
        ends[-1].start()
    for end in ends:
        end.wait()


def whole(*shape):
    return pl.BlockSpec(shape, lambda: (0,) * len(shape))


def struct(*shape):
    return jax.ShapeDtypeStruct(shape, jnp.bfloat16)


LIMIT = 64 * 1024 * 1024 - 64 * 1024
HBM = pl.BlockSpec(memory_space=pltpu.HBM)
LAYER_SCRATCH = [
    pltpu.VMEM((WINDOWS, SPAN, WIDTH), jnp.float32),
    pltpu.VMEM((WINDOWS * SPAN, WIDTH), jnp.bfloat16),
    pltpu.VMEM((WINDOWS * SPAN, WIDTH), jnp.bfloat16),
    pltpu.VMEM((WINDOWS * SPAN, WIDTH), jnp.bfloat16),
    pltpu.VMEM((WINDOWS, WIDTH, SPAN), jnp.bfloat16),
    pltpu.VMEM((2, 4, HEADS // 4 * SPAN, MAIN), jnp.float32),
    pltpu.VMEM((2, HEADS // GROUP, SPAN, MAIN), jnp.float32),
    pltpu.VMEM((2, WIDTH, MAIN), jnp.float32),
    pltpu.VMEM((WIDTH, 3 * WIDTH), jnp.bfloat16),
    pltpu.VMEM((WIDTH, WIDTH), jnp.bfloat16),
    pltpu.SemaphoreType.DMA((2,)),
]
LAYER_SPECS = [HBM, HBM, whole(3, 2, WIDTH)]
LAYER_FLOPS = 2 * 4 * SPAN * (6 * WIDTH * WIDTH + 5 * 8 * SPAN * WIDTH)


def first_layer(pair, tokens, layers, passed):
    counts = (7, 7, 1 + len(passed), 1)
    return pl.pallas_call(
        functools.partial(first_kernel, pair),
        in_specs=[HBM] + LAYER_SPECS + [HBM] * len(passed),
        out_specs=[HBM] * 4,
        out_shape=[struct(n, QUAD, WIDTH) for n in counts],
        scratch_shapes=LAYER_SCRATCH
        + [
            pltpu.VMEM((WINDOWS, WIN, WIN, 4, WIDTH), jnp.bfloat16),
            pltpu.VMEM((2, 8, QUAD, WIDTH), jnp.bfloat16),
            pltpu.SemaphoreType.DMA((WINDOWS,)),
            pltpu.SemaphoreType.DMA((2, 8)),
            pltpu.SemaphoreType.DMA(()),
        ],
        compiler_params=pltpu.CompilerParams(vmem_limit_bytes=LIMIT),
        cost_estimate=pl.CostEstimate(flops=LAYER_FLOPS, bytes_accessed=5 << 20, transcendentals=16 * 4 * SPAN * SPAN),
        name=f"layer0_pair{pair}",
    )(tokens, *layers, *passed)


def second_layer(pair, pieces, layers, w_merge, passed):
    shapes = [(BACK, 2 * WIDTH), (BACK, 2 * WIDTH), (1 + len(passed), SUB, 2 * WIDTH), (1, SUB, 2 * WIDTH)]
    return pl.pallas_call(
        functools.partial(second_kernel, pair),
        in_specs=[HBM] * 4 + LAYER_SPECS + [HBM] + [whole(*p.shape) for p in passed],
        out_specs=[whole(*shape) for shape in shapes],
        out_shape=[struct(*shape) for shape in shapes],
        scratch_shapes=LAYER_SCRATCH
        + [
            pltpu.VMEM((4 * WIDTH, 2 * WIDTH), jnp.bfloat16),
            pltpu.VMEM((2, 8, QUAD, WIDTH), jnp.bfloat16),
            pltpu.VMEM((4, QUAD, 4 * WIDTH), jnp.float32),
            pltpu.SemaphoreType.DMA(()),
            pltpu.SemaphoreType.DMA((4,)),
        ],
        compiler_params=pltpu.CompilerParams(vmem_limit_bytes=LIMIT),
        cost_estimate=pl.CostEstimate(
            flops=LAYER_FLOPS + 2 * SPAN * 8 * WIDTH * WIDTH, bytes_accessed=8 << 20, transcendentals=16 * 4 * SPAN * SPAN
        ),
        name=f"layer1_pair{pair}",
    )(*pieces, *layers, w_merge, *passed)


def moved(value, down, east):
    lats, lons = lax.axis_size("lat"), lax.axis_size("lon")
    pairs = [
        (lat * lons + lon, (lat + down) % lats * lons + (lon + east) % lons) for lat in range(lats) for lon in range(lons)
    ]
    return lax.ppermute(value, ("lat", "lon"), pairs)


def body(tokens, w_qkv, w_out, modulation, w_merge):
    layers = (w_qkv, w_out, jnp.swapaxes(modulation, 0, 1))
    firsts, passed = [], []
    for pair in range(2):
        firsts.append(first_layer(pair, tokens, layers, passed))
        passed = firsts[-1][2:3]
    beside = moved(passed[0], 0, -1)
    placed, passed = [], []
    for pair, (moving, staying, _, corner) in enumerate(firsts):
        way = 2 * pair - 1
        pieces = (staying, moved(moving, way, 0), beside, moved(corner, way, -1))
        away, own, east, corner = second_layer(pair, pieces, layers, w_merge, passed)
        placed += [own, moved(away, -way, 0), moved(corner, -way, 1)]
        passed = [east]
    placed.append(moved(east, 0, 1))
    rows, cols = tokens.shape[0] // 2, tokens.shape[1] // 2
    return pl.pallas_call(
        last_kernel,
        in_specs=[HBM] * len(placed),
        out_specs=HBM,
        out_shape=struct(rows, cols, 4, 2 * WIDTH),
        scratch_shapes=[pltpu.VMEM(p.shape, p.dtype) for p in placed]
        + [
            pltpu.VMEM((rows, cols, 4, 2 * WIDTH), jnp.bfloat16),
            pltpu.SemaphoreType.DMA((len(placed),)),
            pltpu.SemaphoreType.DMA((2,)),
        ],
        compiler_params=pltpu.CompilerParams(vmem_limit_bytes=LIMIT),
        name="placing",
    )(*placed)


def solution(mesh):
    in_specs = (P("lat", "lon", None, None), P(), P(), P(), P())
    out_specs = P("lat", "lon", None, None)
    return jax.shard_map(body, mesh=mesh, in_specs=in_specs, out_specs=out_specs, check_vma=False)
```

```python
import functools
import math

import jax
import jax.numpy as jnp
from jax import lax
from jax.experimental import pallas as pl
from jax.experimental.pallas import tpu as pltpu
from jax.sharding import PartitionSpec as P

HEADS = 16
WIN = 12
HALF = 6
QUAD = 72
SPAN = 4 * QUAD
WIDTH = 512
HEAD = WIDTH // HEADS
GROUP = 8
MAIN = 256
REST = SPAN - MAIN
SUB = 18
WINDOWS = 4
TOGETHER = (4, 1)
BACK = 128
FAR = -1e30
SCALE = math.log2(math.e) / math.sqrt(HEAD)
NT = (((1,), (1,)), ((), ()))


def dot(a, b):
    return jnp.dot(a, b, preferred_element_type=jnp.float32)


def dot_nt(a, b):
    return lax.dot_general(a, b, NT, preferred_element_type=jnp.float32)


def normalized(values, eps):
    centered = values - jnp.mean(values, axis=-1, keepdims=True)
    return centered * lax.rsqrt(jnp.mean(centered * centered, axis=-1, keepdims=True) + eps)


def softened(scores, apart, straddles):
    half = SPAN // 2
    top, bottom = scores[:half], scores[half:]
    most_top, most_bottom = jnp.max(top, axis=0, keepdims=True), jnp.max(bottom, axis=0, keepdims=True)
    if apart is None:
        most_top = most_bottom = jnp.maximum(most_top, most_bottom)
    else:
        if straddles:
            lane = lax.broadcasted_iota(jnp.int32, (1, MAIN), 1)
            from_top = jnp.where(lane < half, 0.0, apart)
            from_bottom = jnp.where(lane < half, apart, 0.0)
        else:
            from_top = jnp.full((1, MAIN), apart, jnp.float32)
            from_bottom = jnp.zeros((1, MAIN), jnp.float32)
        most = jnp.maximum(most_top + from_top, most_bottom + from_bottom)
        most_top, most_bottom = most - from_top, most - from_bottom
    top, bottom = jnp.exp2(top - most_top), jnp.exp2(bottom - most_bottom)
    total = jnp.sum(top, axis=0, keepdims=True) + jnp.sum(bottom, axis=0, keepdims=True)
    return jnp.concatenate([top.astype(jnp.bfloat16), bottom.astype(jnp.bfloat16)], axis=0), 1.0 / total


def attend_windows(together, fill, finish, grid_ref, wqkv_ref, wout_ref, mod_ref, scratch, copies, apart):
    hidden_ref, query_ref, keys_ref, vt_ref, scores_ref, rest_ref, att_ref = scratch
    copy_qkv, copy_out = copies
    wide = GROUP * HEAD
    lane_head = lax.broadcasted_iota(jnp.int32, (1, wide), 1) // HEAD
    same = (
        lax.broadcasted_iota(jnp.int32, (wide, wide), 0) // HEAD
        == lax.broadcasted_iota(jnp.int32, (wide, wide), 1) // HEAD
    )

    def main_rows(w):
        return pl.ds(pl.multiple_of(w * MAIN, MAIN), MAIN)

    def rest_rows(w):
        return pl.ds(pl.multiple_of(WINDOWS * MAIN + w * REST, REST), REST)

    @pl.loop(0, WINDOWS)
    def _(w):
        fill(w)
        hidden = (normalized(grid_ref[w], 1e-06) * (1.0 + mod_ref[0]) + mod_ref[1]).astype(jnp.bfloat16)
        hidden_ref[main_rows(w)] = hidden[:MAIN]
        hidden_ref[rest_rows(w)] = hidden[MAIN:]

    copy_qkv.wait()

    @pl.loop(0, HEADS // GROUP)
    def _(group):
        here = pl.ds(pl.multiple_of(group * wide, wide), wide)
        there = pl.ds(pl.multiple_of(WIDTH + group * wide, wide), wide)
        query_ref[:, here] = (dot(hidden_ref[...], wqkv_ref[:, here]) * SCALE).astype(jnp.bfloat16)
        keys_ref[:, here] = dot(hidden_ref[...], wqkv_ref[:, there]).astype(jnp.bfloat16)

    values = dot_nt(wqkv_ref[:, 2 * WIDTH :].T, hidden_ref[...]).astype(jnp.bfloat16)
    for w in range(WINDOWS):
        vt_ref[w, :, :MAIN] = values[:, w * MAIN : (w + 1) * MAIN]
        vt_ref[w, :, MAIN:] = values[:, WINDOWS * MAIN + w * REST : WINDOWS * MAIN + (w + 1) * REST]

    def attend(w, scores_ref, rest_ref, att_ref):
        for group in range(HEADS // GROUP):
            cols = slice(group * wide, (group + 1) * wide)
            kg = jnp.concatenate([keys_ref[main_rows(w), cols], keys_ref[rest_rows(w), cols]], axis=0)
            qm, qr = query_ref[main_rows(w), cols], query_ref[rest_rows(w), cols]
            for part in range(2):
                items = range(part * GROUP // 2, (part + 1) * GROUP // 2)
                masked = jnp.concatenate([kg * (lane_head == item).astype(jnp.bfloat16) for item in items], axis=0)
                scores_ref[2 * group + part] = dot_nt(masked, qm)
            rest_ref[group] = dot_nt(kg, jnp.concatenate([qr] * GROUP, axis=0) * same.astype(jnp.bfloat16))
        rest = []
        for group in range(HEADS // GROUP):
            cols = slice(group * wide, (group + 1) * wide)
            for item in range(GROUP):
                heads = slice((group * GROUP + item) * HEAD, (group * GROUP + item + 1) * HEAD)
                start = item % (GROUP // 2) * SPAN
                scores = scores_ref[2 * group + item // (GROUP // 2), start : start + SPAN]
                weights, share = softened(scores, apart, True)
                att_ref[heads] = dot(vt_ref[w, heads], weights) * share
            weights, share = softened(rest_ref[group], apart, False)
            mixed = dot(vt_ref[w, cols], weights) * share
            own = [slice(item * HEAD, (item + 1) * HEAD) for item in range(GROUP)]
            rest.append(jnp.concatenate([mixed[part, part] for part in own], axis=0).T.astype(jnp.bfloat16))
        hidden_ref[main_rows(w)] = att_ref[...].T.astype(jnp.bfloat16)
        hidden_ref[rest_rows(w)] = jnp.concatenate(rest, axis=1)

    @pl.loop(0, WINDOWS // together)
    def _(step):
        for index in range(together):
            slot = index % 2
            attend(together * step + index, scores_ref.at[slot], rest_ref.at[slot], att_ref.at[slot])

    copy_out.wait()
    added = (1.0 + mod_ref[2]) * dot(hidden_ref[...], wout_ref[...])
    for w in range(WINDOWS):
        grid_ref[w, :MAIN] += added[w * MAIN : (w + 1) * MAIN]
        grid_ref[w, MAIN:] += added[WINDOWS * MAIN + w * REST : WINDOWS * MAIN + (w + 1) * REST]
        finish(w)


def staged(layer, wqkv_hbm, wout_hbm, wqkv_ref, wout_ref, sems):
    copies = (
        pltpu.make_async_copy(wqkv_hbm.at[layer], wqkv_ref, sems.at[0]),
        pltpu.make_async_copy(wout_hbm.at[layer], wout_ref, sems.at[1]),
    )
    for copy in copies:
        copy.start()
    return copies


def first_kernel(
    pair, tokens_hbm, wqkv_hbm, wout_hbm, mod_ref, *refs,
):
    if pair:
        first_west_hbm, *refs = refs
    moving_hbm, staying_hbm, west_hbm, corner_hbm, grid_ref, *scratch = refs
    *scratch, wqkv_ref, wout_ref, sems, tokens_ref, pieces_ref, token_sems, piece_sems, pass_sem = scratch
    ends = []
    if pair:
        ends.append(pltpu.make_async_copy(first_west_hbm, west_hbm.at[pl.ds(0, 1)], pass_sem))
        ends[-1].start()

    def brought(w):
        columns = pl.ds(w * WIN, WIN)
        return pltpu.make_async_copy(tokens_hbm.at[:, columns], tokens_ref.at[w], token_sems.at[w])

    for w in range(WINDOWS):
        brought(w).start()
    copies = staged(0, wqkv_hbm, wout_hbm, wqkv_ref, wout_ref, sems)

    def fill(w):
        brought(w).wait()
        for quad in range(4):
            for sub in range(4):
                for place in range(9):
                    i = quad // 2 * HALF + place // 3 * 2 + sub % 2
                    j = quad % 2 * HALF + place % 3 * 2 + sub // 2
                    row = quad * QUAD + sub * SUB + place * 2
                    grid_ref[w, row : row + 2] = tokens_ref[w, i, j, 2 * pair : 2 * pair + 2].astype(jnp.float32)

    def finish(w):
        for quad in range(4):
            half, block = quad // 2, 2 * w + quad % 2
            piece = pieces_ref.at[half, pl.ds(block, 1)]
            piece[0] = grid_ref[w, quad * QUAD : (quad + 1) * QUAD].astype(jnp.bfloat16)
            if block:
                target = (moving_hbm if half == pair else staying_hbm).at[pl.ds(block - 1, 1)]
            else:
                target = corner_hbm if half == pair else west_hbm.at[pl.ds(pair, 1)]
            ends.append(pltpu.make_async_copy(piece, target, piece_sems.at[half, block]))
            ends[-1].start()

    attend_windows(TOGETHER[0], fill, finish, grid_ref, wqkv_ref, wout_ref, mod_ref.at[:, pl.ds(0, 1)], scratch, copies, None)
    for end in ends:
        end.wait()


def second_kernel(
    pair, staying_hbm, received_hbm, east_hbm, corner_hbm, wqkv_hbm, wout_hbm, mod_ref, merge_hbm, *refs,
):
    if pair:
        first_east_ref, *refs = refs
    away_ref, own_ref, back_east_ref, corner_ref, grid_ref, *scratch = refs
    if pair:
        back_east_ref[0] = first_east_ref[0]
    *scratch, wqkv_ref, wout_ref, sems, merge_ref, pieces_ref, joined_ref, flat_ref, merged_ref, merge_sem, piece_sems = scratch
    kept, got = pieces_ref.at[pair], pieces_ref.at[1 - pair]
    begins = [
        pltpu.make_async_copy(source, target, piece_sems.at[index])
        for index, (source, target) in enumerate(
            [
                (staying_hbm, kept.at[pl.ds(0, 7)]),
                (received_hbm, got.at[pl.ds(0, 7)]),
                (east_hbm.at[pl.ds(pair, 1)], kept.at[pl.ds(7, 1)]),
                (corner_hbm, got.at[pl.ds(7, 1)]),
            ]
        )
    ]
    for begin in begins:
        begin.start()
    copies = staged(1, wqkv_hbm, wout_hbm, wqkv_ref, wout_ref, sems)
    copy_merge = pltpu.make_async_copy(merge_hbm, merge_ref, merge_sem)
    copy_merge.start()
    for begin in begins:
        begin.wait()

    def fill(w):
        for quad in range(4):
            grid_ref[w, quad * QUAD : (quad + 1) * QUAD] = pieces_ref[quad // 2, 2 * w + quad % 2].astype(jnp.float32)

    def finish(w):
        for quad in range(4):
            for sub in range(4):
                start = quad * QUAD + sub * SUB
                joined_ref[w, quad * SUB : (quad + 1) * SUB, sub * WIDTH : (sub + 1) * WIDTH] = (
                    grid_ref[w, start : start + SUB].astype(jnp.bfloat16).astype(jnp.float32)
                )

    border = 0 if pair else lax.axis_size("lat") - 1
    apart = jnp.where(lax.axis_index("lat") == border, FAR, 0.0)
    attend_windows(TOGETHER[1], fill, finish, grid_ref, wqkv_ref, wout_ref, mod_ref.at[:, pl.ds(1, 1)], scratch, copies, apart)
    @pl.loop(0, WINDOWS)
    def _(w):
        joined_ref[w] = normalized(joined_ref[w], 1e-05)

    flat_ref[...] = jnp.concatenate([joined_ref[w].astype(jnp.bfloat16) for w in range(WINDOWS)], axis=0)
    copy_merge.wait()

    @pl.loop(0, 4)
    def _(part):
        here = pl.ds(pl.multiple_of(part * WIDTH // 2, WIDTH // 2), WIDTH // 2)
        merged_ref[:, here] = dot(flat_ref[...], merge_ref[:, here])

    merged = merged_ref
    for half in range(2):
        target, last = (own_ref, back_east_ref) if half == pair else (away_ref, corner_ref)
        rows = [merged[w * QUAD + 2 * half * SUB : w * QUAD + 2 * (half + 1) * SUB, :] for w in range(WINDOWS)]
        rows = jnp.concatenate(rows, axis=0)
        target[...] = rows[:BACK].astype(jnp.bfloat16)
        last[last.shape[0] - 1] = rows[7 * SUB :].astype(jnp.bfloat16)


def last_kernel(*refs):
    count = len(refs) // 2 - 2
    sources, out_hbm, held, (out_ref, sems, out_sems) = refs[:count], refs[count], refs[count + 1 : -3], refs[-3:]
    copies = [pltpu.make_async_copy(*pair, sems.at[index]) for index, pair in enumerate(zip(sources, held))]
    for copy in copies:
        copy.start()
    for copy in copies:
        copy.wait()
    ends = []
    for half in range(2):
        for pair in range(2):
            own, back, corner = held[3 * pair : 3 * pair + 3]
            for block in range(8):
                if half != pair:
                    ref = own if block else held[-1].at[pair]
                else:
                    ref = back if block else corner.at[0]
                for place in range(9):
                    i, j = half * 3 + place // 3, block * 3 + place % 3
                    row = max(block - 1, 0) * SUB + 2 * place
                    out_ref[i, j, 2 * pair : 2 * pair + 2] = ref[row : row + 2]
        rows = pl.ds(half * 3, 3)
        ends.append(pltpu.make_async_copy(out_ref.at[rows], out_hbm.at[rows], out_sems.at[half]))
        ends[-1].start()
    for end in ends:
        end.wait()


def whole(*shape):
    return pl.BlockSpec(shape, lambda: (0,) * len(shape))


def struct(*shape):
    return jax.ShapeDtypeStruct(shape, jnp.bfloat16)


LIMIT = 64 * 1024 * 1024 - 64 * 1024
HBM = pl.BlockSpec(memory_space=pltpu.HBM)
LAYER_SCRATCH = [
    pltpu.VMEM((WINDOWS, SPAN, WIDTH), jnp.float32),
    pltpu.VMEM((WINDOWS * SPAN, WIDTH), jnp.bfloat16),
    pltpu.VMEM((WINDOWS * SPAN, WIDTH), jnp.bfloat16),
    pltpu.VMEM((WINDOWS * SPAN, WIDTH), jnp.bfloat16),
    pltpu.VMEM((WINDOWS, WIDTH, SPAN), jnp.bfloat16),
    pltpu.VMEM((2, 4, HEADS // 4 * SPAN, MAIN), jnp.float32),
    pltpu.VMEM((2, HEADS // GROUP, SPAN, MAIN), jnp.float32),
    pltpu.VMEM((2, WIDTH, MAIN), jnp.float32),
    pltpu.VMEM((WIDTH, 3 * WIDTH), jnp.bfloat16),
    pltpu.VMEM((WIDTH, WIDTH), jnp.bfloat16),
    pltpu.SemaphoreType.DMA((2,)),
]
LAYER_SPECS = [HBM, HBM, whole(3, 2, WIDTH)]
LAYER_FLOPS = 2 * 4 * SPAN * (6 * WIDTH * WIDTH + 5 * 8 * SPAN * WIDTH)


def first_layer(pair, tokens, layers, passed):
    counts = (7, 7, 1 + len(passed), 1)
    return pl.pallas_call(
        functools.partial(first_kernel, pair),
        in_specs=[HBM] + LAYER_SPECS + [HBM] * len(passed),
        out_specs=[HBM] * 4,
        out_shape=[struct(n, QUAD, WIDTH) for n in counts],
        scratch_shapes=LAYER_SCRATCH
        + [
            pltpu.VMEM((WINDOWS, WIN, WIN, 4, WIDTH), jnp.bfloat16),
            pltpu.VMEM((2, 8, QUAD, WIDTH), jnp.bfloat16),
            pltpu.SemaphoreType.DMA((WINDOWS,)),
            pltpu.SemaphoreType.DMA((2, 8)),
            pltpu.SemaphoreType.DMA(()),
        ],
        compiler_params=pltpu.CompilerParams(vmem_limit_bytes=LIMIT),
        cost_estimate=pl.CostEstimate(flops=LAYER_FLOPS, bytes_accessed=5 << 20, transcendentals=16 * 4 * SPAN * SPAN),
        name=f"layer0_pair{pair}",
    )(tokens, *layers, *passed)


def second_layer(pair, pieces, layers, w_merge, passed):
    shapes = [(BACK, 2 * WIDTH), (BACK, 2 * WIDTH), (1 + len(passed), SUB, 2 * WIDTH), (1, SUB, 2 * WIDTH)]
    return pl.pallas_call(
        functools.partial(second_kernel, pair),
        in_specs=[HBM] * 4 + LAYER_SPECS + [HBM] + [whole(*p.shape) for p in passed],
        out_specs=[whole(*shape) for shape in shapes],
        out_shape=[struct(*shape) for shape in shapes],
        scratch_shapes=LAYER_SCRATCH
        + [
            pltpu.VMEM((4 * WIDTH, 2 * WIDTH), jnp.bfloat16),
            pltpu.VMEM((2, 8, QUAD, WIDTH), jnp.bfloat16),
            pltpu.VMEM((4, QUAD, 4 * WIDTH), jnp.float32),
            pltpu.VMEM((SPAN, 4 * WIDTH), jnp.bfloat16),
            pltpu.VMEM((SPAN, 2 * WIDTH), jnp.float32),
            pltpu.SemaphoreType.DMA(()),
            pltpu.SemaphoreType.DMA((4,)),
        ],
        compiler_params=pltpu.CompilerParams(vmem_limit_bytes=LIMIT),
        cost_estimate=pl.CostEstimate(
            flops=LAYER_FLOPS + 2 * SPAN * 8 * WIDTH * WIDTH, bytes_accessed=8 << 20, transcendentals=16 * 4 * SPAN * SPAN
        ),
        name=f"layer1_pair{pair}",
    )(*pieces, *layers, w_merge, *passed)


def moved(value, down, east):
    lats, lons = lax.axis_size("lat"), lax.axis_size("lon")
    pairs = [
        (lat * lons + lon, (lat + down) % lats * lons + (lon + east) % lons) for lat in range(lats) for lon in range(lons)
    ]
    return lax.ppermute(value, ("lat", "lon"), pairs)


def body(tokens, w_qkv, w_out, modulation, w_merge):
    layers = (w_qkv, w_out, jnp.swapaxes(modulation, 0, 1))
    firsts, passed = [], []
    for pair in range(2):
        firsts.append(first_layer(pair, tokens, layers, passed))
        passed = firsts[-1][2:3]
    beside = moved(passed[0], 0, -1)
    placed, passed = [], []
    for pair, (moving, staying, _, corner) in enumerate(firsts):
        way = 2 * pair - 1
        pieces = (staying, moved(moving, way, 0), beside, moved(corner, way, -1))
        away, own, east, corner = second_layer(pair, pieces, layers, w_merge, passed)
        placed += [own, moved(away, -way, 0), moved(corner, -way, 1)]
        passed = [east]
    placed.append(moved(east, 0, 1))
    rows, cols = tokens.shape[0] // 2, tokens.shape[1] // 2
    return pl.pallas_call(
        last_kernel,
        in_specs=[HBM] * len(placed),
        out_specs=HBM,
        out_shape=struct(rows, cols, 4, 2 * WIDTH),
        scratch_shapes=[pltpu.VMEM(p.shape, p.dtype) for p in placed]
        + [
            pltpu.VMEM((rows, cols, 4, 2 * WIDTH), jnp.bfloat16),
            pltpu.SemaphoreType.DMA((len(placed),)),
            pltpu.SemaphoreType.DMA((2,)),
        ],
        compiler_params=pltpu.CompilerParams(vmem_limit_bytes=LIMIT),
        name="placing",
    )(*placed)


def solution(mesh):
    in_specs = (P("lat", "lon", None, None), P(), P(), P(), P())
    out_specs = P("lat", "lon", None, None)
    return jax.shard_map(body, mesh=mesh, in_specs=in_specs, out_specs=out_specs, check_vma=False)
```
